512 devices in a mesh: dp: 4 (over x), expert: 128 (over z, y, core).
Axes of the slice: x: 4, y: 8, z: 8, core: 2. Of those that a mesh axis runs over, the one named last changes fastest.
Arguments:
- tokens: bfloat16 [12288, 1024], P(('dp', 'expert')), may hold values from -6 to 6
- grad_out: bfloat16 [12288, 1024], P(('dp', 'expert')), may hold values from -6 to 6
- expert_ids: int32 [12288, 8], P(('dp', 'expert')), may hold values from 0 to 127, all different within a row; in each aligned block of 24 rows (0 to 23, 24 to 47, ...) at most 2 rows name the same one
- gates: float32 [12288, 8], P(('dp', 'expert')), may hold values from 0.05 to 0.5
- w_in: bfloat16 [128, 1024, 2, 512], P('expert', None, None, 'dp'), may hold values from -0.1875 to 0.1875
- w_out: bfloat16 [128, 512, 1024], P('expert', 'dp'), may hold values from -0.25 to 0.25
Outputs:
- mixed: bfloat16 [12288, 1024], P(('dp', 'expert'))
- grad_tokens: bfloat16 [12288, 1024], P(('dp', 'expert'))
- grad_gates: float32 [12288, 8], P(('dp', 'expert'))
- grad_w_in: float32 [128, 1024, 2, 512], P('expert', None, None, 'dp')
- grad_w_out: float32 [128, 512, 1024], P('expert', 'dp')
The draws below stay inside these ranges and needn't reach their ends.
Inputs may be any that keep to these rules, and one draw needn't show every extreme that they name: `expert_ids`: each token names 8 different experts; the rows of one device name no expert more than 2 times, a bound that some block reaches.
All inputs are finite; a program needn't handle non-finite values.
Results may differ from the reference program's by a relative error of at most 0.012.
Values may be sent and summed in bfloat16 or wider, within the bound.
No kernel may reach another device: no remote copies, remote signals or barrier semaphores. Data moves between devices by JAX's collectives and lax.ppermute only.
A program may use at most 64 MiB of HBM per device.

```python
import math
import jax
import jax.numpy as jnp
import numpy as np
from jax import lax

D = 1024
H = 512
TOP = 8
TOK_DEV = 24
EXPERTS = 128
CAP = 2
TOKENS = 12288
N_DP = 4
N_EXPERT = 128


def shard_levels(rng, shape, shards, low, high):
    factor_of = 1.0
    for dim, parts in shards:
        heights = jax.random.uniform(jax.random.fold_in(jax.random.fold_in(rng, 6), dim), (parts,), jnp.float32, low / len(shards), high / len(shards))
        factor_of = factor_of * jnp.repeat(jnp.exp(heights), shape[dim] // parts).reshape((-1,) + (1,) * (len(shape) - 1 - dim))
    return factor_of


def shared_out(rng, own, number, rows, number_of, top, limit, lean):
    order = jax.random.permutation(rng, number_of)
    crowded, ordinary = load_shares(number_of, rows * top, limit, lean, True), load_shares(number_of, rows * top, limit, lean, False)
    places = jnp.arange(number_of)

    def named(sizes, turn):
        used = int((sizes > 0).sum())
        fixed = max(1, used // 4)
        shifted = fixed + (places - fixed + turn * (used - fixed)) % max(1, number_of - fixed)
        return jnp.zeros((number_of,), jnp.int32).at[order[jnp.where(places < fixed, places, shifted)]].set(jnp.asarray(sizes, jnp.int32))

    sizes = jnp.where(number % 4 == 0, named(crowded, number // 4), named(ordinary, number - number // 4 - 1))
    mixed = jax.random.permutation(jax.random.fold_in(own, 3), number_of)
    source_of, taker = mixed[0:number_of // 2 * 2:2], mixed[1:number_of // 2 * 2:2]
    margin = jnp.minimum(sizes[source_of] - 1, limit - sizes[taker]) // 2
    margin = jnp.where((source_of == order[0]) | (taker == order[0]) | (sizes[taker] == 0), 0, jnp.maximum(margin, 0))
    shifted = jax.random.randint(jax.random.fold_in(own, 4), (number_of // 2,), 0, 1 << 20) % (margin + 1)
    sizes = sizes.at[source_of].add(-shifted).at[taker].add(shifted)
    labels = jnp.searchsorted(jnp.cumsum(sizes), jnp.arange(rows * top), side="right").astype(jnp.int32)
    listing = labels.reshape(top, rows).T
    listing = listing[jax.random.permutation(jax.random.fold_in(own, 1), rows)]
    turn = jax.random.randint(jax.random.fold_in(own, 2), (rows, 1), 0, top)
    return jnp.take_along_axis(listing, (jnp.arange(top)[None, :] + turn) % top, axis=1)


def load_shares(number_of, total, reach, lean, full):
    loads = [(1 << 20) // math.isqrt(grade ** lean) + 1 for grade in range(1, number_of + 1)]
    largest = reach if full else min(reach, max(-(-total // number_of), total * loads[0] // sum(loads)))
    least = 1 if total - largest >= number_of - 1 else 0
    given, surplus = [largest] + [least] * (number_of - 1), total - largest - least * (number_of - 1)
    while surplus > 0:
        free = [i for i in range(1, number_of) if given[i] < largest] or [i for i in range(1, number_of) if given[i] < reach]
        whole, left = sum([loads[i] for i in free]), surplus
        for i in free:
            addition = min(reach - given[i], max(1, left * loads[i] // whole), surplus)
            given[i] = given[i] + addition
            surplus = surplus - addition
    return np.array(given)


def noise(own_key, extent, deviation, bound, split=(), kind=jnp.bfloat16):
    factor_of = shard_levels(own_key, extent, split, -0.22, 0.18) if split else 1.0
    values = jax.random.normal(own_key, extent, jnp.float32) * deviation * factor_of
    return jnp.minimum(jnp.maximum(values, -bound), bound).astype(kind)


def setup_inputs(seed: int = 0) -> dict:
    streams_of = jax.random.split(jax.random.key(seed), 7)
    tokens = noise(streams_of[0], (TOKENS, D), 1.0, 6.0, ((0, 512),))
    grad_out = noise(streams_of[1], (TOKENS, D), 1.0, 6.0, ((0, 512),))
    expert_ids_keys = jax.random.split(jax.random.fold_in(streams_of[2], 1), TOKENS // TOK_DEV)
    expert_ids_turns = jax.random.permutation(jax.random.fold_in(streams_of[2], 3), TOKENS // TOK_DEV)
    expert_ids = jax.vmap(lambda own, number: shared_out(jax.random.fold_in(streams_of[2], 2), own, number, TOK_DEV, EXPERTS, TOP, CAP, 2))(expert_ids_keys, expert_ids_turns).reshape((TOKENS, TOP))
    gates = jnp.clip(jnp.exp(math.log(0.5) - 2.3025851 * jax.random.uniform(streams_of[3], (TOKENS, TOP), jnp.float32) ** shard_levels(streams_of[3], (TOKENS, TOP), ((0, 512),), -0.2, 0.2)), 0.05, 0.5)
    w_in = noise(streams_of[4], (EXPERTS, D, 2, H), D ** -0.5, 0.1875, ((0, 128), (3, 4)))
    w_out = noise(streams_of[5], (EXPERTS, H, D), H ** -0.5, 0.25, ((0, 128), (1, 4)))
    return {"tokens": tokens, "grad_out": grad_out, "expert_ids": expert_ids, "gates": gates, "w_in": w_in, "w_out": w_out}


def expert_pass(rows, grad_rows, weight_in, weight_out):
    model_width = rows.shape[1]
    hidden_width = weight_out.shape[0]
    flat_in = weight_in.reshape(model_width, 2 * hidden_width)
    preact = jnp.dot(rows, flat_in, preferred_element_type=jnp.float32)
    gate_part = preact[:, :hidden_width]
    up_part = preact[:, hidden_width:]
    sigmoid_gate = jax.nn.sigmoid(gate_part)
    activated = gate_part * sigmoid_gate
    hidden = (activated * up_part).astype(jnp.bfloat16)
    result = jnp.dot(hidden, weight_out, preferred_element_type=jnp.float32).astype(jnp.bfloat16)
    back_grad = jnp.dot(grad_rows, weight_out.T, preferred_element_type=jnp.float32)
    grad_gate = back_grad * up_part * (sigmoid_gate * (1.0 + gate_part * (1.0 - sigmoid_gate)))
    grad_up = back_grad * activated
    grad_pre = jnp.concatenate([grad_gate, grad_up], axis=1).astype(jnp.bfloat16)
    grad_rows_in = jnp.dot(grad_pre, flat_in.T, preferred_element_type=jnp.float32).astype(jnp.bfloat16)
    grad_weight_in = jnp.dot(rows.T, grad_pre, preferred_element_type=jnp.float32)
    grad_weight_out = jnp.dot(hidden.T, grad_rows, preferred_element_type=jnp.float32)
    return result, grad_rows_in, grad_weight_in, grad_weight_out


def reference(tokens, grad_out, expert_ids, gates, w_in, w_out):
    group_size = TOK_DEV * N_EXPERT
    row_count = group_size * TOP
    slot_count = N_EXPERT * CAP
    model_width = tokens.shape[1]
    hidden_width = w_out.shape[1]

    def expert_step(running, inputs):
        out_sum, grad_sum, gate_grad = running
        expert, weight_in, weight_out = inputs
        grad_in_sum = jnp.zeros((model_width, 2 * hidden_width), jnp.float32)
        grad_out_sum = jnp.zeros((hidden_width, model_width), jnp.float32)
        for replica in range(N_DP):
            lower = replica * group_size
            group_tokens = lax.slice_in_dim(tokens, lower, lower + group_size)
            group_grad = lax.slice_in_dim(grad_out, lower, lower + group_size)
            group_ids = lax.slice_in_dim(expert_ids, lower, lower + group_size)
            group_gates = lax.slice_in_dim(gates, lower, lower + group_size)
            flat_ids = group_ids.reshape(-1)
            positions = jnp.nonzero(flat_ids == expert, size=slot_count, fill_value=row_count)[0].astype(jnp.int32)
            valid_row = positions < row_count
            safe_rows = jnp.minimum(positions, row_count - 1).astype(jnp.int32)
            token_pos = (safe_rows // TOP).astype(jnp.int32)
            slot_k = (safe_rows % TOP).astype(jnp.int32)
            rows = jnp.where(valid_row[:, None], group_tokens[token_pos], jnp.zeros((), jnp.bfloat16))
            weight_gate = jnp.where(valid_row, group_gates[token_pos, slot_k], jnp.zeros((), jnp.float32))
            cotangent = group_grad[token_pos].astype(jnp.float32)
            grad_rows = (weight_gate[:, None] * cotangent).astype(jnp.bfloat16)
            result, grad_rows_in, grad_weight_in, grad_weight_out = expert_pass(rows, grad_rows, weight_in, weight_out)
            result_wide = result.astype(jnp.float32)
            out_sum = out_sum.at[replica, token_pos].add(weight_gate[:, None] * result_wide)
            grad_sum = grad_sum.at[replica, token_pos].add(grad_rows_in.astype(jnp.float32))
            gate_term = jnp.where(valid_row, jnp.sum(cotangent * result_wide, axis=1), jnp.zeros((), jnp.float32))
            gate_grad = gate_grad.at[replica, token_pos, slot_k].add(gate_term)
            grad_in_sum = grad_in_sum + lax.optimization_barrier(grad_weight_in.astype(jnp.bfloat16)).astype(jnp.float32)
            grad_out_sum = grad_out_sum + lax.optimization_barrier(grad_weight_out.astype(jnp.bfloat16)).astype(jnp.float32)
        stacked = grad_in_sum.reshape(model_width, 2, hidden_width)
        return (out_sum, grad_sum, gate_grad), (stacked, grad_out_sum)

    start = (jnp.zeros((N_DP, group_size, model_width), jnp.float32),
             jnp.zeros((N_DP, group_size, model_width), jnp.float32),
             jnp.zeros((N_DP, group_size, TOP), jnp.float32))
    experts_list = jnp.arange(N_EXPERT, dtype=jnp.int32)
    finals, stacked_grads = lax.scan(expert_step, start, (experts_list, w_in, w_out))
    out_sum, grad_sum, gate_grad = finals
    mixed = out_sum.reshape(TOKENS, model_width).astype(jnp.bfloat16)
    grad_tokens = grad_sum.reshape(TOKENS, model_width).astype(jnp.bfloat16)
    grad_gates = gate_grad.reshape(TOKENS, TOP)
    return mixed, grad_tokens, grad_gates, stacked_grads[0], stacked_grads[1]
```

```python
import jax
import jax.numpy as jnp
from jax import lax
from jax.experimental import pallas as pl
from jax.experimental.pallas import tpu as pltpu
from jax.sharding import PartitionSpec as P

BF16 = jnp.bfloat16
F32 = jnp.float32
SLOTS = 2
VMEM_LIMIT = 48 * 1024 * 1024


def routing(ids, gates, groups):
    count_tok, per_token = ids.shape
    slots = groups * SLOTS
    lane = lax.broadcasted_iota(jnp.int32, (count_tok, slots), 1)
    expert = lane // SLOTS
    place = lane % SLOTS
    named = jnp.zeros((count_tok, slots), F32)
    gate = jnp.zeros((count_tok, slots), F32)
    for k in range(per_token):
        hit = ids[:, k : k + 1] == expert
        named = jnp.where(hit, 1.0, named)
        gate = jnp.where(hit, gates[:, k : k + 1], gate)
    row = lax.broadcasted_iota(jnp.int32, (count_tok, count_tok), 0)
    col = lax.broadcasted_iota(jnp.int32, (count_tok, count_tok), 1)
    earlier = (col < row).astype(BF16)
    rank = jnp.dot(earlier, named.astype(BF16), preferred_element_type=F32)
    held = jnp.where(rank == place.astype(F32), named, 0.0)
    return held, held * gate, expert


def three_parts(x):
    high = x.astype(BF16)
    rest = x - high.astype(F32)
    mid = rest.astype(BF16)
    low = (rest - mid.astype(F32)).astype(BF16)
    return high, mid, low


def dispatch_kernel(tokens_ref, grad_ref, ids_ref, gates_ref, send_ref):
    model = tokens_ref.shape[1]
    groups = send_ref.shape[0] // SLOTS
    held, gate, _ = routing(ids_ref[...], gates_ref[...], groups)
    pick = (((0,), (0,)), ((), ()))
    send_ref[:, :model] = lax.dot_general(
        held.astype(BF16), tokens_ref[...], pick, preferred_element_type=F32
    ).astype(BF16)
    grad = grad_ref[...]
    send_ref[:, model:] = lax.dot_general(
        jnp.concatenate(three_parts(gate), axis=0),
        jnp.concatenate([grad, grad, grad], axis=0),
        pick,
        preferred_element_type=F32,
    ).astype(BF16)


def expert_kernel(model, *refs):
    pieces = (len(refs) - 2) // 2
    rows_ref, weights = refs[0], refs[1 : 1 + pieces]
    back_ref, grads = refs[1 + pieces], refs[2 + pieces :]
    rows = rows_ref[:, :model]
    grad_rows = rows_ref[:, model:]
    last = (((1,), (1,)), ((), ()))
    first = (((0,), (0,)), ((), ()))
    result = None
    dx = None
    for w_ref, g_ref in zip(weights, grads):
        wide = w_ref.shape[1]
        width = wide // 2
        w_in = w_ref[:model, :]
        w_out = jnp.concatenate(
            [w_ref[model + i * width : model + (i + 1) * width, :] for i in range(model // wide)], axis=1
        )
        preact = jnp.dot(rows, w_in, preferred_element_type=F32)
        gate_part, up_part = preact[:, :width], preact[:, width:]
        sig = jax.nn.sigmoid(gate_part)
        activated = gate_part * sig
        hidden = (activated * up_part).astype(BF16)
        back = lax.dot_general(grad_rows, w_out, last, preferred_element_type=F32)
        grad_gate = back * up_part * (sig * (1.0 + gate_part * (1.0 - sig)))
        grad_pre = jnp.concatenate([grad_gate, back * activated], axis=1).astype(BF16)
        part = jnp.dot(hidden, w_out, preferred_element_type=F32)
        result = part if result is None else result + part
        part = lax.dot_general(grad_pre, w_in, last, preferred_element_type=F32)
        dx = part if dx is None else dx + part
        g_ref[:model, :] = lax.dot_general(rows, grad_pre, first, preferred_element_type=F32).astype(BF16)
        grad_out = lax.dot_general(hidden, grad_rows, first, preferred_element_type=F32).astype(BF16)
        for i in range(model // wide):
            g_ref[model + i * width : model + (i + 1) * width, :] = grad_out[:, i * wide : (i + 1) * wide]
    back_ref[:, :model] = result.astype(BF16)
    back_ref[:, model:] = dx.astype(BF16)


def combine_kernel(back_ref, grad_ref, ids_ref, gates_ref, mixed_ref, dx_ref, gate_grad_ref):
    model = grad_ref.shape[1]
    groups = back_ref.shape[0] // SLOTS
    ids = ids_ref[...]
    count_tok, per_token = ids.shape
    held, gate, expert = routing(ids, gates_ref[...], groups)
    result = back_ref[:, :model]
    mixed = jnp.dot(jnp.concatenate(three_parts(gate), axis=0), result, preferred_element_type=F32)
    mixed_ref[...] = (
        mixed[:count_tok] + mixed[count_tok : 2 * count_tok] + mixed[2 * count_tok :]
    ).astype(BF16)
    dx_ref[...] = jnp.dot(held.astype(BF16), back_ref[:, model:], preferred_element_type=F32).astype(BF16)
    inner = lax.dot_general(grad_ref[...], result, (((1,), (1,)), ((), ())), preferred_element_type=F32)
    inner = inner * held
    for k in range(per_token):
        hit = ids[:, k : k + 1] == expert
        gate_grad_ref[:, k : k + 1] = jnp.sum(jnp.where(hit, inner, 0.0), axis=1, keepdims=True)


def per_device(tokens, grad_out, expert_ids, gates, w_in, w_out):
    count_tok, model = tokens.shape
    groups = lax.axis_size("expert")
    replicas = lax.axis_size("dp")
    width = w_out.shape[1]
    wide = 2 * width
    params = pltpu.CompilerParams(vmem_limit_bytes=VMEM_LIMIT)

    def shift(x, by):
        return lax.ppermute(x, "dp", [(i, (i + by) % replicas) for i in range(replicas)])

    packed = jnp.concatenate(
        [
            w_in.reshape(model, wide),
            w_out.reshape(width, model // wide, wide).transpose(1, 0, 2).reshape(-1, wide),
        ],
        axis=0,
    )
    order = (0, 1, 3, 2)
    weights = [packed] + [shift(packed, -s) for s in order[1:]]

    send = pl.pallas_call(
        dispatch_kernel,
        out_shape=jax.ShapeDtypeStruct((groups * SLOTS, 2 * model), BF16),
        compiler_params=params,
        name="dispatch",
    )(tokens, grad_out, expert_ids, gates)

    def exchange(x):
        x = x.reshape(groups, SLOTS, 2 * model)
        x = lax.all_to_all(x, "expert", split_axis=0, concat_axis=0, tiled=True)
        return x.reshape(groups * SLOTS, 2 * model)

    arrived = exchange(send)
    back, *grads = pl.pallas_call(
        lambda *refs: expert_kernel(model, *refs),
        out_shape=[jax.ShapeDtypeStruct((groups * SLOTS, 2 * model), BF16)]
        + [jax.ShapeDtypeStruct(packed.shape, BF16)] * replicas,
        compiler_params=params,
        name="expert",
    )(arrived, *weights)
    total = grads[0].astype(F32)
    for s, grad in zip(order[1:], grads[1:]):
        total = total + shift(grad, s).astype(F32)
    returned = exchange(back)
    mixed, grad_tokens, grad_gates = pl.pallas_call(
        combine_kernel,
        out_shape=[
            jax.ShapeDtypeStruct(tokens.shape, BF16),
            jax.ShapeDtypeStruct(tokens.shape, BF16),
            jax.ShapeDtypeStruct(gates.shape, F32),
        ],
        compiler_params=params,
        name="combine",
    )(returned, grad_out, expert_ids, gates)
    grad_w_in = total[:model].reshape(1, model, 2, width)
    grad_w_out = total[model:].reshape(model // wide, width, wide).transpose(1, 0, 2).reshape(1, width, model)
    return mixed, grad_tokens, grad_gates, grad_w_in, grad_w_out


def solution(mesh):
    in_specs = (
        P(("dp", "expert"), None),
        P(("dp", "expert"), None),
        P(("dp", "expert"), None),
        P(("dp", "expert"), None),
        P("expert", None, None, "dp"),
        P("expert", "dp", None),
    )
    out_specs = (
        P(("dp", "expert"), None),
        P(("dp", "expert"), None),
        P(("dp", "expert"), None),
        P("expert", None, None, "dp"),
        P("expert", "dp", None),
    )
    return jax.shard_map(
        per_device, mesh=mesh, in_specs=in_specs, out_specs=out_specs, check_vma=False
    )
```

```python
import jax
import jax.numpy as jnp
from jax import lax
from jax.experimental import pallas as pl
from jax.experimental.pallas import tpu as pltpu
from jax.sharding import PartitionSpec as P

BF16 = jnp.bfloat16
F32 = jnp.float32
SLOTS = 2
PIECE = 8
PEERS = 16
VMEM_LIMIT = 20 * 1024 * 1024
KEEP = int(1.9e10)
BESIDE = int(2e11)
FIRST = (((0,), (0,)), ((), ()))
LAST = (((1,), (1,)), ((), ()))


def routing(ids, gates, groups):
    per_token, count_tok = ids.shape
    slots = groups * SLOTS
    line = lax.broadcasted_iota(jnp.int32, (slots, count_tok), 0)
    expert = line % groups
    place = line // groups
    named = jnp.zeros((slots, count_tok), F32)
    gate = jnp.zeros((slots, count_tok), F32)
    for k in range(per_token):
        hit = ids[k : k + 1, :] == expert
        named = jnp.where(hit, 1.0, named)
        gate = jnp.where(hit, gates[k : k + 1, :], gate)
    row = lax.broadcasted_iota(jnp.int32, (count_tok, count_tok), 0)
    col = lax.broadcasted_iota(jnp.int32, (count_tok, count_tok), 1)
    earlier = (row < col).astype(BF16)
    rank = jnp.dot(named.astype(BF16), earlier, preferred_element_type=F32)
    held = jnp.where(rank == place.astype(F32), named, 0.0)
    return held, held * gate, expert


def three_parts(x):
    high = x.astype(BF16)
    rest = x - high.astype(F32)
    mid = rest.astype(BF16)
    low = (rest - mid.astype(F32)).astype(BF16)
    return high, mid, low


def weave(back):
    size = PEERS * PIECE
    major, minor = (PIECE, PEERS) if back else (PEERS, PIECE)
    row = lax.broadcasted_iota(jnp.int32, (size, size), 0)
    col = lax.broadcasted_iota(jnp.int32, (size, size), 1)
    return ((row % minor) * major + row // minor == col).astype(BF16)


def weave_blocks(first, second, wire_ref):
    groups = first.shape[0] // SLOTS
    half = first.shape[1] // 2
    size = PEERS * PIECE
    permute = weave(False)
    for b in range(groups // PEERS):
        parts = []
        for array in (first, second):
            for c in range(SLOTS):
                lines = array[c * groups + b * PEERS : c * groups + (b + 1) * PEERS]
                parts += [lines[:, :half], lines[:, half:]]
        wire_ref[b * size : (b + 1) * size, :] = jnp.dot(
            permute, jnp.concatenate(parts, axis=0), preferred_element_type=F32
        ).astype(BF16)


def unweave_blocks(wire_ref, first_ref, second_ref):
    groups = first_ref.shape[0] // SLOTS
    half = first_ref.shape[1] // 2
    size = PEERS * PIECE
    permute = weave(True)
    for b in range(groups // PEERS):
        lines = jnp.dot(
            permute, wire_ref[b * size : (b + 1) * size, :], preferred_element_type=F32
        ).astype(BF16)
        i = 0
        for ref in (first_ref, second_ref):
            for c in range(SLOTS):
                for h in range(2):
                    ref[c * groups + b * PEERS : c * groups + (b + 1) * PEERS, h * half : (h + 1) * half] = lines[
                        i * PEERS : (i + 1) * PEERS
                    ]
                    i += 1


def start_all(pairs, sem):
    copies = [pltpu.make_async_copy(source, target, sem.at[i]) for i, (source, target) in enumerate(pairs)]
    for copy in copies:
        copy.start()
    return copies


def wait_all(copies):
    for copy in copies:
        copy.wait()


def dispatch_kernel(
    in_hbm, out_hbm, tokens_hbm, grad_hbm, ids_hbm, gates_hbm, packed_hbm, send_hbm,
    raw_ref, packed_ref, tokens_ref, grad_ref, ids_ref, gates_ref, wire_ref, sem, wire_sem,
):
    model = in_hbm.shape[0]
    groups = send_hbm.shape[0] // PIECE
    wide = packed_ref.shape[1]
    width = wide // 2
    pairs = [(ids_hbm, ids_ref), (gates_hbm, gates_ref), (in_hbm, raw_ref)]
    for i in range(model // wide):
        pairs.append(
            (
                out_hbm.at[:, i * wide : (i + 1) * wide],
                packed_ref.at[model + i * width : model + (i + 1) * width, :],
            )
        )
    pairs += [(tokens_hbm, tokens_ref), (grad_hbm, grad_ref)]
    copies = start_all(pairs, sem)
    copies[0].wait()
    copies[1].wait()
    held, gate, _ = routing(ids_ref[...], gates_ref[...], groups)
    wait_all(copies[2:-2])
    raw = raw_ref[...]
    packed_ref[:model, :width] = raw[:, 0, :]
    packed_ref[:model, width:] = raw[:, 1, :]
    leaving = pltpu.make_async_copy(packed_ref, packed_hbm, sem.at[0])
    leaving.start()
    wait_all(copies[-2:])
    rows = jnp.dot(held.astype(BF16), tokens_ref[...], preferred_element_type=F32).astype(BF16)
    grad = grad_ref[...]
    grad_rows = jnp.dot(
        jnp.concatenate(three_parts(gate), axis=1),
        jnp.concatenate([grad, grad, grad], axis=0),
        preferred_element_type=F32,
    ).astype(BF16)
    weave_blocks(rows, grad_rows, wire_ref)
    sending = pltpu.make_async_copy(wire_ref, send_hbm, wire_sem)
    sending.start()
    leaving.wait()
    sending.wait()


def assembly(sources, in_ref, out_ref):
    model = in_ref.shape[0]
    wide = sources[0].shape[1]
    width = wide // 2
    pairs = []
    for r, source in enumerate(sources):
        pairs.append((source.at[:model, :], in_ref.at[:, r * wide : (r + 1) * wide]))
        for i in range(model // wide):
            pairs.append(
                (
                    source.at[model + i * width : model + (i + 1) * width, :],
                    out_ref.at[r * width : (r + 1) * width, i * wide : (i + 1) * wide],
                )
            )
    return pairs


def weight_grads(rows, grad_rows, hidden, grad_pre, r, grad_ref):
    model = rows.shape[1]
    wide = grad_ref.shape[1]
    width = wide // 2
    grad_ref[:model, :] = lax.dot_general(
        rows, grad_pre[:, r * wide : (r + 1) * wide], FIRST, preferred_element_type=F32
    ).astype(BF16)
    value = lax.dot_general(
        hidden[:, r * width : (r + 1) * width], grad_rows, FIRST, preferred_element_type=F32
    ).astype(BF16)
    for i in range(model // wide):
        grad_ref[model + i * width : model + (i + 1) * width, :] = value[:, i * wide : (i + 1) * wide]


def expert_kernel(
    pieces, wire_hbm, *refs
):
    sources, back_hbm, grads_hbm = refs[:pieces], refs[pieces], refs[pieces + 1 : 2 * pieces + 1]
    grads = refs[2 * pieces + 1 : 3 * pieces + 1]
    (
        in_ref, out_ref, wire_ref, rows_ref, grad_rows_ref, hidden_ref, grad_pre_ref, sem, weights_sem, grad_sem
    ) = refs[3 * pieces + 1 :]
    wide = grads[0].shape[1]
    width = wide // 2
    arriving = pltpu.make_async_copy(wire_hbm, wire_ref, sem)
    arriving.start()
    weights = start_all(assembly(sources, in_ref, out_ref), weights_sem)
    arriving.wait()
    unweave_blocks(wire_ref, rows_ref, grad_rows_ref)
    wait_all(weights)
    rows = rows_ref[...]
    grad_rows = grad_rows_ref[...]
    preact = jnp.dot(rows, in_ref[...], preferred_element_type=F32)
    back = lax.dot_general(grad_rows, out_ref[...], LAST, preferred_element_type=F32)
    for r in range(pieces):
        gate_part = preact[:, r * wide : r * wide + width]
        up_part = preact[:, r * wide + width : (r + 1) * wide]
        back_part = back[:, r * width : (r + 1) * width]
        sig = jax.nn.sigmoid(gate_part)
        activated = gate_part * sig
        grad_gate = back_part * up_part * (sig * (1.0 + gate_part * (1.0 - sig)))
        hidden_ref[:, r * width : (r + 1) * width] = (activated * up_part).astype(BF16)
        grad_pre_ref[:, r * wide : r * wide + width] = grad_gate.astype(BF16)
        grad_pre_ref[:, r * wide + width : (r + 1) * wide] = (back_part * activated).astype(BF16)
    hidden = hidden_ref[...]
    grad_pre = grad_pre_ref[...]
    result = jnp.dot(hidden, out_ref[...], preferred_element_type=F32).astype(BF16)
    dx = lax.dot_general(grad_pre, in_ref[...], LAST, preferred_element_type=F32).astype(BF16)
    weave_blocks(result, dx, wire_ref)
    sending = pltpu.make_async_copy(wire_ref, back_hbm, sem)
    sending.start()
    order = (1, 2, 3, 0)
    for r in order:
        weight_grads(rows, grad_rows, hidden, grad_pre, r, grads[r])
    leaving = start_all([(grads[r], grads_hbm[r]) for r in order], grad_sem)
    sending.wait()
    wait_all(leaving)


def finish_kernel(
    wire_hbm, grad_hbm, ids_hbm, gates_hbm, partial_any, next_any, last_any,
    mixed_ref, dx_ref, gate_grad_ref, in_hbm, out_hbm,
    wire_ref, result_ref, back_ref, grad_ref, ids_ref, gates_ref,
    partial_ref, next_ref, last_ref, in_ref, out_ref, sem, out_sem,
):
    groups = result_ref.shape[0] // SLOTS
    model = result_ref.shape[1]
    wide = next_ref.shape[1]
    width = wide // 2
    copies = start_all(
        [(ids_hbm, ids_ref), (gates_hbm, gates_ref), (partial_any, partial_ref), (next_any, next_ref)]
        + [(last_any, last_ref), (grad_hbm, grad_ref), (wire_hbm, wire_ref)],
        sem,
    )
    wait_all(copies[:2])
    ids = ids_ref[...]
    per_token, count_tok = ids.shape
    held, gate, expert = routing(ids, gates_ref[...], groups)
    mix = jnp.concatenate([part.astype(F32) for part in three_parts(gate)] + [held], axis=1).T.astype(BF16)

    def total(lower, size):
        value = partial_ref[lower : lower + size, :]
        for piece in (next_ref, last_ref):
            value = value + piece[lower : lower + size, :].astype(F32)
        return value

    wait_all(copies[2:])
    value = total(0, model)
    in_ref[pl.ds(0, model, stride=2), :] = value[:, :width]
    in_ref[pl.ds(1, model, stride=2), :] = value[:, width:]
    for i in range(model // wide):
        out_ref[:, i * wide : (i + 1) * wide] = total(model + i * width, width)
    leaving = start_all([(in_ref, in_hbm), (out_ref, out_hbm)], out_sem)
    unweave_blocks(wire_ref, result_ref, back_ref)
    result = result_ref[...]
    gate_rows = 3 * count_tok
    mixed = jnp.dot(mix[:gate_rows], result, preferred_element_type=F32)
    mixed_ref[...] = (
        mixed[:count_tok] + mixed[count_tok : 2 * count_tok] + mixed[2 * count_tok :]
    ).astype(BF16)
    dx_ref[...] = jnp.dot(mix[gate_rows:], back_ref[...], preferred_element_type=F32).astype(BF16)
    inner = lax.dot_general(result, grad_ref[...], LAST, preferred_element_type=F32) * held
    for k in range(per_token):
        hit = ids[k : k + 1, :] == expert
        gate_grad_ref[k : k + 1, :] = jnp.sum(jnp.where(hit, inner, 0.0), axis=0, keepdims=True)
    wait_all(leaving)


def add_kernel(first_ref, second_ref, total_ref):
    total_ref[...] = first_ref[...].astype(F32) + second_ref[...].astype(F32)


def per_device(tokens, grad_out, expert_ids, gates, w_in, w_out):
    count_tok, model = tokens.shape
    per_token = gates.shape[1]
    groups = lax.axis_size("expert")
    replicas = lax.axis_size("dp")
    width = w_out.shape[1]
    wide = 2 * width
    slots = groups * SLOTS
    wire = jax.ShapeDtypeStruct((groups * PIECE, model // 2), BF16)
    params = pltpu.CompilerParams(vmem_limit_bytes=VMEM_LIMIT)
    in_hbm = pl.BlockSpec(memory_space=pltpu.HBM)
    anywhere = pl.BlockSpec(memory_space=pl.ANY)
    in_vmem = pl.BlockSpec(memory_space=pltpu.VMEM)
    small = pltpu.CompilerParams(vmem_limit_bytes=4 * 1024 * 1024)

    def shift(x, by):
        return lax.ppermute(x, "dp", [(i, (i + by) % replicas) for i in range(replicas)])

    def held_in(x, space):
        return pltpu.with_memory_space_constraint(x, space)

    def exchange(x):
        x = x.reshape(groups, PIECE, model // 2)
        x = lax.all_to_all(x, "expert", split_axis=0, concat_axis=0, tiled=True)
        return x.reshape(groups * PIECE, model // 2)

    ids_t, gates_t = expert_ids.T, gates.T
    tokens_like = pltpu.VMEM(tokens.shape, BF16)
    ids_like = pltpu.VMEM(ids_t.shape, jnp.int32)
    gates_like = pltpu.VMEM(gates_t.shape, F32)
    piece = (model + width * (model // wide), wide)
    piece_like = pltpu.VMEM(piece, BF16)
    rows_like = pltpu.VMEM((slots, model), BF16)
    hidden_like = pltpu.VMEM((slots, replicas * width), BF16)
    grad_pre_like = pltpu.VMEM((slots, replicas * wide), BF16)
    wire_like = pltpu.VMEM(wire.shape, BF16)
    lines = 1 + model // wide
    inputs = [w_in.reshape(model, 2, width), w_out.reshape(width, model), tokens, grad_out, ids_t, gates_t]
    packed, send = pl.pallas_call(
        dispatch_kernel,
        out_shape=[pltpu.HBM(piece, BF16), pltpu.HBM(wire.shape, BF16)],
        in_specs=[in_hbm] * 6,
        out_specs=[in_hbm] * 2,
        scratch_shapes=[
            pltpu.VMEM((model, 2, width), BF16),
            piece_like, tokens_like, tokens_like, ids_like, gates_like, wire_like,
            pltpu.SemaphoreType.DMA((lines + 4,)),
            pltpu.SemaphoreType.DMA,
        ],
        compiler_params=params,
        name="dispatch",
    )(*[held_in(x, pltpu.HBM) for x in inputs])
    far = shift(packed, -2)
    far_late = pl.pallas_call(
        lambda far_hbm, out_ref, sem: wait_all(start_all([(far_hbm, out_ref)], sem)),
        out_shape=piece_like,
        in_specs=[anywhere],
        scratch_shapes=[pltpu.SemaphoreType.DMA((1,))],
        compiler_params=small,
        cost_estimate=pl.CostEstimate(flops=KEEP, bytes_accessed=0, transcendentals=0),
        name="keep",
    )(far)
    arrived = exchange(send)

    back, own, grad_far, grad_next, grad_last = pl.pallas_call(
        lambda *refs: expert_kernel(replicas, *refs),
        out_shape=[pltpu.HBM(wire.shape, BF16)] + [pltpu.HBM(piece, BF16)] * replicas,
        in_specs=[in_hbm] + [anywhere] * replicas,
        out_specs=[in_hbm] * (1 + replicas),
        scratch_shapes=[piece_like] * replicas
        + [
            pltpu.VMEM((model, replicas * wide), BF16),
            pltpu.VMEM((replicas * width, model), BF16),
            wire_like, rows_like, rows_like, hidden_like, grad_pre_like,
            pltpu.SemaphoreType.DMA,
            pltpu.SemaphoreType.DMA((replicas * lines,)),
            pltpu.SemaphoreType.DMA((replicas,)),
        ],
        compiler_params=params,
        name="expert",
    )(arrived, held_in(packed, pltpu.HBM), far_late, shift(packed, -1), shift(packed, 1))
    returned = exchange(back)
    partial = pl.pallas_call(
        add_kernel,
        out_shape=jax.ShapeDtypeStruct(piece, F32),
        compiler_params=params,
        cost_estimate=pl.CostEstimate(flops=BESIDE, bytes_accessed=0, transcendentals=0),
        name="add",
    )(own, shift(grad_far, 2))
    mixed, grad_tokens, gate_grad, sum_in, sum_out = pl.pallas_call(
        finish_kernel,
        out_shape=[
            jax.ShapeDtypeStruct(tokens.shape, BF16),
            jax.ShapeDtypeStruct(tokens.shape, BF16),
            jax.ShapeDtypeStruct((per_token, count_tok), F32),
            pltpu.HBM((2 * model, width), F32),
            pltpu.HBM((width, model), F32),
        ],
        in_specs=[in_hbm] * 4 + [anywhere] * 3,
        out_specs=[in_vmem] * 3 + [in_hbm] * 2,
        scratch_shapes=[
            wire_like, rows_like, rows_like, tokens_like, ids_like, gates_like,
            pltpu.VMEM(piece, F32), piece_like, piece_like,
            pltpu.VMEM((2 * model, width), F32),
            pltpu.VMEM((width, model), F32),
            pltpu.SemaphoreType.DMA((7,)),
            pltpu.SemaphoreType.DMA((2,)),
        ],
        compiler_params=params,
        name="finish",
    )(
        returned, *[held_in(x, pltpu.HBM) for x in (grad_out, ids_t, gates_t)],
        partial, shift(grad_next, 1), shift(grad_last, -1),
    )
    return mixed, grad_tokens, gate_grad.T, sum_in.reshape(1, model, 2, width), sum_out[None]


def solution(mesh):
    in_specs = (
        P(("dp", "expert"), None),
        P(("dp", "expert"), None),
        P(("dp", "expert"), None),
        P(("dp", "expert"), None),
        P("expert", None, None, "dp"),
        P("expert", "dp", None),
    )
    out_specs = (
        P(("dp", "expert"), None),
        P(("dp", "expert"), None),
        P(("dp", "expert"), None),
        P("expert", None, None, "dp"),
        P("expert", "dp", None),
    )
    return jax.shard_map(
        per_device, mesh=mesh, in_specs=in_specs, out_specs=out_specs, check_vma=False
    )
```

```python
import jax
import jax.numpy as jnp
from jax import lax
from jax.experimental import pallas as pl
from jax.experimental.pallas import tpu as pltpu
from jax.sharding import PartitionSpec as P

BF16 = jnp.bfloat16
F32 = jnp.float32
SLOTS = 2
PIECE = 8
PEERS = 16
MIB = 1024 * 1024
KEEP = int(1.9e10)
BESIDE = int(1e11)
FIRST = (((0,), (0,)), ((), ()))
LAST = (((1,), (1,)), ((), ()))


def routing(ids, gates, groups):
    per_token, count_tok = ids.shape
    slots = groups * SLOTS
    line = lax.broadcasted_iota(jnp.int32, (slots, count_tok), 0)
    expert = line % groups
    place = line // groups
    named = jnp.zeros((slots, count_tok), F32)
    gate = jnp.zeros((slots, count_tok), F32)
    for k in range(per_token):
        hit = ids[k : k + 1, :] == expert
        named = jnp.where(hit, 1.0, named)
        gate = jnp.where(hit, gates[k : k + 1, :], gate)
    row = lax.broadcasted_iota(jnp.int32, (count_tok, count_tok), 0)
    col = lax.broadcasted_iota(jnp.int32, (count_tok, count_tok), 1)
    earlier = (row < col).astype(BF16)
    rank = jnp.dot(named.astype(BF16), earlier, preferred_element_type=F32)
    held = jnp.where(rank == place.astype(F32), named, 0.0)
    return held, held * gate, expert


def three_parts(x):
    high = x.astype(BF16)
    rest = x - high.astype(F32)
    mid = rest.astype(BF16)
    low = (rest - mid.astype(F32)).astype(BF16)
    return high, mid, low


def weave(back):
    size = PEERS * PIECE
    major, minor = (PIECE, PEERS) if back else (PEERS, PIECE)
    row = lax.broadcasted_iota(jnp.int32, (size, size), 0)
    col = lax.broadcasted_iota(jnp.int32, (size, size), 1)
    return ((row % minor) * major + row // minor == col).astype(BF16)


def weave_blocks(first, second, wire_ref):
    groups = first.shape[0] // SLOTS
    half = first.shape[1] // 2
    size = PEERS * PIECE
    permute = weave(False)
    for b in range(groups // PEERS):
        parts = []
        for array in (first, second):
            for c in range(SLOTS):
                lines = array[c * groups + b * PEERS : c * groups + (b + 1) * PEERS]
                parts += [lines[:, :half], lines[:, half:]]
        wire_ref[b * size : (b + 1) * size, :] = jnp.dot(
            permute, jnp.concatenate(parts, axis=0), preferred_element_type=F32
        ).astype(BF16)


def unweave_blocks(wire_ref, first_ref, second_ref):
    groups = first_ref.shape[0] // SLOTS
    half = first_ref.shape[1] // 2
    size = PEERS * PIECE
    permute = weave(True)
    for b in range(groups // PEERS):
        lines = jnp.dot(
            permute, wire_ref[b * size : (b + 1) * size, :], preferred_element_type=F32
        ).astype(BF16)
        i = 0
        for ref in (first_ref, second_ref):
            for c in range(SLOTS):
                for h in range(2):
                    ref[c * groups + b * PEERS : c * groups + (b + 1) * PEERS, h * half : (h + 1) * half] = lines[
                        i * PEERS : (i + 1) * PEERS
                    ]
                    i += 1


def start_all(pairs, sem):
    copies = [pltpu.make_async_copy(source, target, sem.at[i]) for i, (source, target) in enumerate(pairs)]
    for copy in copies:
        copy.start()
    return copies


def wait_all(copies):
    for copy in copies:
        copy.wait()


def dispatch_kernel(
    in_hbm, out_hbm, tokens_hbm, grad_hbm, ids_hbm, gates_hbm, packed_hbm, send_hbm,
    raw_ref, packed_ref, tokens_ref, grad_ref, ids_ref, gates_ref, wire_ref, sem, wire_sem,
):
    model = in_hbm.shape[0]
    groups = send_hbm.shape[0] // PIECE
    wide = packed_ref.shape[1]
    width = wide // 2
    pairs = [(ids_hbm, ids_ref), (gates_hbm, gates_ref), (tokens_hbm, tokens_ref), (grad_hbm, grad_ref)]
    small = len(pairs)
    pairs.append((in_hbm, raw_ref))
    for i in range(model // wide):
        pairs.append(
            (
                out_hbm.at[:, i * wide : (i + 1) * wide],
                packed_ref.at[model + i * width : model + (i + 1) * width, :],
            )
        )
    copies = start_all(pairs, sem)
    wait_all(copies[:small])
    held, gate, _ = routing(ids_ref[...], gates_ref[...], groups)
    rows = jnp.dot(held.astype(BF16), tokens_ref[...], preferred_element_type=F32).astype(BF16)
    grad = grad_ref[...]
    grad_rows = jnp.dot(
        jnp.concatenate(three_parts(gate), axis=1),
        jnp.concatenate([grad, grad, grad], axis=0),
        preferred_element_type=F32,
    ).astype(BF16)
    weave_blocks(rows, grad_rows, wire_ref)
    sending = pltpu.make_async_copy(wire_ref, send_hbm, wire_sem)
    sending.start()
    wait_all(copies[small:])
    packed_ref[:model, :] = raw_ref[...].reshape(model, wide)
    leaving = pltpu.make_async_copy(packed_ref, packed_hbm, sem.at[0])
    leaving.start()
    sending.wait()
    leaving.wait()


def assembly(sources, in_ref, out_ref):
    model = in_ref.shape[0]
    wide = sources[0].shape[1]
    width = wide // 2
    pairs = []
    for r, source in enumerate(sources):
        pairs.append((source.at[:model, :], in_ref.at[:, r * wide : (r + 1) * wide]))
        for i in range(model // wide):
            pairs.append(
                (
                    source.at[model + i * width : model + (i + 1) * width, :],
                    out_ref.at[r * width : (r + 1) * width, i * wide : (i + 1) * wide],
                )
            )
    return pairs


def weight_grads(rows, grad_rows, hidden, grad_pre, r, grad_ref):
    model = rows.shape[1]
    wide = grad_ref.shape[1]
    width = wide // 2
    grad_ref[:model, :] = lax.dot_general(
        rows, grad_pre[:, r * wide : (r + 1) * wide], FIRST, preferred_element_type=F32
    ).astype(BF16)
    value = lax.dot_general(
        hidden[:, r * width : (r + 1) * width], grad_rows, FIRST, preferred_element_type=F32
    ).astype(BF16)
    for i in range(model // wide):
        grad_ref[model + i * width : model + (i + 1) * width, :] = value[:, i * wide : (i + 1) * wide]


def expert_kernel(
    pieces, wire_hbm, *refs
):
    sources, back_hbm, grads_hbm = refs[:pieces], refs[pieces], refs[pieces + 1 : 2 * pieces + 1]
    grads = refs[2 * pieces + 1 : 3 * pieces + 1]
    (
        in_ref, out_ref, wire_ref, rows_ref, grad_rows_ref, hidden_ref, grad_pre_ref, sem, weights_sem, grad_sem
    ) = refs[3 * pieces + 1 :]
    wide = grads[0].shape[1]
    width = wide // 2
    arriving = pltpu.make_async_copy(wire_hbm, wire_ref, sem)
    arriving.start()
    weights = start_all(assembly(sources, in_ref, out_ref), weights_sem)
    arriving.wait()
    unweave_blocks(wire_ref, rows_ref, grad_rows_ref)
    wait_all(weights)
    rows = rows_ref[...]
    grad_rows = grad_rows_ref[...]
    preact = jnp.dot(rows, in_ref[...], preferred_element_type=F32)
    back = lax.dot_general(grad_rows, out_ref[...], LAST, preferred_element_type=F32)
    for r in range(pieces):
        gate_part = preact[:, r * wide : r * wide + width]
        up_part = preact[:, r * wide + width : (r + 1) * wide]
        back_part = back[:, r * width : (r + 1) * width]
        sig = jax.nn.sigmoid(gate_part)
        activated = gate_part * sig
        grad_gate = back_part * up_part * (sig * (1.0 + gate_part * (1.0 - sig)))
        hidden_ref[:, r * width : (r + 1) * width] = (activated * up_part).astype(BF16)
        grad_pre_ref[:, r * wide : r * wide + width] = grad_gate.astype(BF16)
        grad_pre_ref[:, r * wide + width : (r + 1) * wide] = (back_part * activated).astype(BF16)
    hidden = hidden_ref[...]
    grad_pre = grad_pre_ref[...]
    order = (1, 2, 3, 0)
    for r in order:
        weight_grads(rows, grad_rows, hidden, grad_pre, r, grads[r])
    leaving = start_all([(grads[r], grads_hbm[r]) for r in order], grad_sem)
    result = jnp.dot(hidden, out_ref[...], preferred_element_type=F32).astype(BF16)
    dx = lax.dot_general(grad_pre, in_ref[...], LAST, preferred_element_type=F32).astype(BF16)
    weave_blocks(result, dx, wire_ref)
    sending = pltpu.make_async_copy(wire_ref, back_hbm, sem)
    sending.start()
    sending.wait()
    wait_all(leaving)


def combine_kernel(
    wire_hbm, grad_hbm, ids_hbm, gates_hbm, mixed_ref, dx_ref, gate_grad_ref,
    wire_ref, result_ref, back_ref, grad_ref, ids_ref, gates_ref, sem,
):
    groups = result_ref.shape[0] // SLOTS
    copies = start_all(
        [(ids_hbm, ids_ref), (gates_hbm, gates_ref), (grad_hbm, grad_ref), (wire_hbm, wire_ref)], sem
    )
    wait_all(copies[:2])
    ids = ids_ref[...]
    per_token, count_tok = ids.shape
    held, gate, expert = routing(ids, gates_ref[...], groups)
    mix = jnp.concatenate([part.astype(F32) for part in three_parts(gate)] + [held], axis=1).T.astype(BF16)
    wait_all(copies[2:])
    unweave_blocks(wire_ref, result_ref, back_ref)
    result = result_ref[...]
    gate_rows = 3 * count_tok
    mixed = jnp.dot(mix[:gate_rows], result, preferred_element_type=F32)
    mixed_ref[...] = (
        mixed[:count_tok] + mixed[count_tok : 2 * count_tok] + mixed[2 * count_tok :]
    ).astype(BF16)
    dx_ref[...] = jnp.dot(mix[gate_rows:], back_ref[...], preferred_element_type=F32).astype(BF16)
    inner = lax.dot_general(result, grad_ref[...], LAST, preferred_element_type=F32) * held
    for k in range(per_token):
        hit = ids[k : k + 1, :] == expert
        gate_grad_ref[k : k + 1, :] = jnp.sum(jnp.where(hit, inner, 0.0), axis=0, keepdims=True)


def add_kernel(first_ref, second_ref, total_ref):
    total_ref[...] = (first_ref[...].astype(F32) + second_ref[...].astype(F32)).astype(BF16)


def reduce_kernel(*refs):
    pieces, (in_ref, out_ref) = refs[:-2], refs[-2:]
    wide = pieces[0].shape[1]
    width = wide // 2
    model = in_ref.shape[0] // 2

    def total(lower, size):
        value = pieces[0][lower : lower + size, :].astype(F32)
        for piece in pieces[1:]:
            value = value + piece[lower : lower + size, :].astype(F32)
        return value

    value = total(0, model)
    in_ref[pl.ds(0, model, stride=2), :] = value[:, :width]
    in_ref[pl.ds(1, model, stride=2), :] = value[:, width:]
    for i in range(model // wide):
        out_ref[:, i * wide : (i + 1) * wide] = total(model + i * width, width)


def per_device(tokens, grad_out, expert_ids, gates, w_in, w_out):
    count_tok, model = tokens.shape
    per_token = gates.shape[1]
    groups = lax.axis_size("expert")
    replicas = lax.axis_size("dp")
    width = w_out.shape[1]
    wide = 2 * width
    slots = groups * SLOTS
    wire = jax.ShapeDtypeStruct((groups * PIECE, model // 2), BF16)
    in_hbm = pl.BlockSpec(memory_space=pltpu.HBM)
    anywhere = pl.BlockSpec(memory_space=pl.ANY)
    in_vmem = pl.BlockSpec(memory_space=pltpu.VMEM)

    def room(mib):
        return pltpu.CompilerParams(vmem_limit_bytes=mib * MIB)


    def shift(x, by):
        return lax.ppermute(x, "dp", [(i, (i + by) % replicas) for i in range(replicas)])

    def held_in(x, space):
        return pltpu.with_memory_space_constraint(x, space)

    def exchange(x):
        x = x.reshape(groups, PIECE, model // 2)
        x = lax.all_to_all(x, "expert", split_axis=0, concat_axis=0, tiled=True)
        return x.reshape(groups * PIECE, model // 2)

    ids_t, gates_t = expert_ids.T, gates.T
    tokens_like = pltpu.VMEM(tokens.shape, BF16)
    ids_like = pltpu.VMEM(ids_t.shape, jnp.int32)
    gates_like = pltpu.VMEM(gates_t.shape, F32)
    piece = (model + width * (model // wide), wide)
    piece_like = pltpu.VMEM(piece, BF16)
    rows_like = pltpu.VMEM((slots, model), BF16)
    hidden_like = pltpu.VMEM((slots, replicas * width), BF16)
    grad_pre_like = pltpu.VMEM((slots, replicas * wide), BF16)
    wire_like = pltpu.VMEM(wire.shape, BF16)
    lines = 1 + model // wide
    inputs = [w_in.reshape(model, 2, width), w_out.reshape(width, model), tokens, grad_out, ids_t, gates_t]
    packed, send = pl.pallas_call(
        dispatch_kernel,
        out_shape=[pltpu.HBM(piece, BF16), pltpu.HBM(wire.shape, BF16)],
        in_specs=[in_hbm] * 6,
        out_specs=[in_hbm] * 2,
        scratch_shapes=[
            pltpu.VMEM((model, 2, width), BF16),
            piece_like, tokens_like, tokens_like, ids_like, gates_like, wire_like,
            pltpu.SemaphoreType.DMA((lines + 4,)),
            pltpu.SemaphoreType.DMA,
        ],
        compiler_params=room(10),
        name="dispatch",
    )(*[held_in(x, pltpu.HBM) for x in inputs])
    far = shift(packed, -2)
    far_late = pl.pallas_call(
        lambda far_hbm, out_ref, sem: wait_all(start_all([(far_hbm, out_ref)], sem)),
        out_shape=piece_like,
        in_specs=[anywhere],
        scratch_shapes=[pltpu.SemaphoreType.DMA((1,))],
        compiler_params=room(4),
        cost_estimate=pl.CostEstimate(flops=KEEP, bytes_accessed=0, transcendentals=0),
        name="keep",
    )(far)
    arrived = exchange(send)

    back, own, grad_far, grad_next, grad_last = pl.pallas_call(
        lambda *refs: expert_kernel(replicas, *refs),
        out_shape=[pltpu.HBM(wire.shape, BF16)] + [pltpu.HBM(piece, BF16)] * replicas,
        in_specs=[in_hbm] + [anywhere] * replicas,
        out_specs=[in_hbm] * (1 + replicas),
        scratch_shapes=[piece_like] * replicas
        + [
            pltpu.VMEM((model, replicas * wide), BF16),
            pltpu.VMEM((replicas * width, model), BF16),
            wire_like, rows_like, rows_like, hidden_like, grad_pre_like,
            pltpu.SemaphoreType.DMA,
            pltpu.SemaphoreType.DMA((replicas * lines,)),
            pltpu.SemaphoreType.DMA((replicas,)),
        ],
        compiler_params=room(20),
        name="expert",
    )(arrived, held_in(packed, pltpu.HBM), far_late, shift(packed, -1), shift(packed, 1))
    returned = exchange(back)
    partial = pl.pallas_call(
        add_kernel,
        out_shape=jax.ShapeDtypeStruct(piece, BF16),
        compiler_params=room(6),
        cost_estimate=pl.CostEstimate(flops=BESIDE, bytes_accessed=0, transcendentals=0),
        name="add",
    )(own, shift(grad_far, 2))
    mixed, grad_tokens, gate_grad = pl.pallas_call(
        combine_kernel,
        out_shape=[
            jax.ShapeDtypeStruct(tokens.shape, BF16),
            jax.ShapeDtypeStruct(tokens.shape, BF16),
            jax.ShapeDtypeStruct((per_token, count_tok), F32),
        ],
        in_specs=[in_hbm] * 4,
        scratch_shapes=[
            wire_like, rows_like, rows_like, tokens_like, ids_like, gates_like,
            pltpu.SemaphoreType.DMA((4,)),
        ],
        compiler_params=room(8),
        name="combine",
    )(returned, *[held_in(x, pltpu.HBM) for x in (grad_out, ids_t, gates_t)])
    partial, mixed = lax.optimization_barrier((partial, mixed))
    sum_in, sum_out = pl.pallas_call(
        reduce_kernel,
        out_shape=[
            jax.ShapeDtypeStruct((2 * model, width), F32),
            jax.ShapeDtypeStruct((width, model), F32),
        ],
        compiler_params=room(8),
        name="reduce",
    )(partial, shift(grad_next, 1), shift(grad_last, -1))
    return mixed, grad_tokens, gate_grad.T, sum_in.reshape(1, model, 2, width), sum_out[None]


def solution(mesh):
    in_specs = (
        P(("dp", "expert"), None),
        P(("dp", "expert"), None),
        P(("dp", "expert"), None),
        P(("dp", "expert"), None),
        P("expert", None, None, "dp"),
        P("expert", "dp", None),
    )
    out_specs = (
        P(("dp", "expert"), None),
        P(("dp", "expert"), None),
        P(("dp", "expert"), None),
        P("expert", None, None, "dp"),
        P("expert", "dp", None),
    )
    return jax.shard_map(
        per_device, mesh=mesh, in_specs=in_specs, out_specs=out_specs, check_vma=False
    )
```

```python
import jax
import jax.numpy as jnp
from jax import lax
from jax.experimental import pallas as pl
from jax.experimental.pallas import tpu as pltpu
from jax.sharding import PartitionSpec as P

BF16 = jnp.bfloat16
F32 = jnp.float32
SLOTS = 2
PIECE = 8
PEERS = 16
MIB = 1024 * 1024
KEEP = int(1.9e10)
BESIDE = int(1e11)
FIRST = (((0,), (0,)), ((), ()))
LAST = (((1,), (1,)), ((), ()))


def routing(ids, gates, groups):
    per_token, count_tok = ids.shape
    slots = groups * SLOTS
    line = lax.broadcasted_iota(jnp.int32, (slots, count_tok), 0)
    expert = line % groups
    place = line // groups
    named = jnp.zeros((slots, count_tok), F32)
    gate = jnp.zeros((slots, count_tok), F32)
    for k in range(per_token):
        hit = ids[k : k + 1, :] == expert
        named = jnp.where(hit, 1.0, named)
        gate = jnp.where(hit, gates[k : k + 1, :], gate)
    row = lax.broadcasted_iota(jnp.int32, (count_tok, count_tok), 0)
    col = lax.broadcasted_iota(jnp.int32, (count_tok, count_tok), 1)
    earlier = (row < col).astype(BF16)
    rank = jnp.dot(named.astype(BF16), earlier, preferred_element_type=F32)
    held = jnp.where(rank == place.astype(F32), named, 0.0)
    return held, held * gate, expert


def three_parts(x):
    high = x.astype(BF16)
    rest = x - high.astype(F32)
    mid = rest.astype(BF16)
    low = (rest - mid.astype(F32)).astype(BF16)
    return high, mid, low


def weave(back):
    size = PEERS * PIECE
    major, minor = (PIECE, PEERS) if back else (PEERS, PIECE)
    row = lax.broadcasted_iota(jnp.int32, (size, size), 0)
    col = lax.broadcasted_iota(jnp.int32, (size, size), 1)
    return ((row % minor) * major + row // minor == col).astype(BF16)


def weave_blocks(first, second, wire_ref):
    groups = first.shape[0] // SLOTS
    half = first.shape[1] // 2
    size = PEERS * PIECE
    permute = weave(False)
    for b in range(groups // PEERS):
        parts = []
        for array in (first, second):
            for c in range(SLOTS):
                lines = array[c * groups + b * PEERS : c * groups + (b + 1) * PEERS]
                parts += [lines[:, :half], lines[:, half:]]
        wire_ref[b * size : (b + 1) * size, :] = jnp.dot(
            permute, jnp.concatenate(parts, axis=0), preferred_element_type=F32
        ).astype(BF16)


def unweave_blocks(wire_ref, first_ref, second_ref):
    groups = first_ref.shape[0] // SLOTS
    half = first_ref.shape[1] // 2
    size = PEERS * PIECE
    permute = weave(True)
    for b in range(groups // PEERS):
        lines = jnp.dot(
            permute, wire_ref[b * size : (b + 1) * size, :], preferred_element_type=F32
        ).astype(BF16)
        i = 0
        for ref in (first_ref, second_ref):
            for c in range(SLOTS):
                for h in range(2):
                    ref[c * groups + b * PEERS : c * groups + (b + 1) * PEERS, h * half : (h + 1) * half] = lines[
                        i * PEERS : (i + 1) * PEERS
                    ]
                    i += 1


def start_all(pairs, sem):
    copies = [pltpu.make_async_copy(source, target, sem.at[i]) for i, (source, target) in enumerate(pairs)]
    for copy in copies:
        copy.start()
    return copies


def wait_all(copies):
    for copy in copies:
        copy.wait()


def dispatch_kernel(
    in_hbm, out_hbm, tokens_hbm, grad_hbm, ids_hbm, gates_hbm, packed_hbm, send_hbm,
    raw_ref, packed_ref, tokens_ref, grad_ref, ids_ref, gates_ref, wire_ref, sem, wire_sem,
):
    model = in_hbm.shape[0]
    groups = send_hbm.shape[0] // PIECE
    wide = packed_ref.shape[1]
    width = wide // 2
    pairs = [(ids_hbm, ids_ref), (gates_hbm, gates_ref), (tokens_hbm, tokens_ref), (grad_hbm, grad_ref)]
    small = len(pairs)
    pairs.append((in_hbm, raw_ref))
    for i in range(model // wide):
        pairs.append(
            (
                out_hbm.at[:, i * wide : (i + 1) * wide],
                packed_ref.at[model + i * width : model + (i + 1) * width, :],
            )
        )
    copies = start_all(pairs, sem)
    wait_all(copies[:small])
    held, gate, _ = routing(ids_ref[...], gates_ref[...], groups)
    rows = jnp.dot(held.astype(BF16), tokens_ref[...], preferred_element_type=F32).astype(BF16)
    grad = grad_ref[...]
    grad_rows = jnp.dot(
        jnp.concatenate(three_parts(gate), axis=1),
        jnp.concatenate([grad, grad, grad], axis=0),
        preferred_element_type=F32,
    ).astype(BF16)
    weave_blocks(rows, grad_rows, wire_ref)
    sending = pltpu.make_async_copy(wire_ref, send_hbm, wire_sem)
    sending.start()
    wait_all(copies[small:])
    packed_ref[:model, :] = raw_ref[...].reshape(model, wide)
    leaving = pltpu.make_async_copy(packed_ref, packed_hbm, sem.at[0])
    leaving.start()
    sending.wait()
    leaving.wait()


def assembly(sources, in_ref, out_ref):
    model = in_ref.shape[0]
    wide = sources[0].shape[1]
    width = wide // 2
    pairs = []
    for r, source in enumerate(sources):
        pairs.append((source.at[:model, :], in_ref.at[:, r * wide : (r + 1) * wide]))
        for i in range(model // wide):
            pairs.append(
                (
                    source.at[model + i * width : model + (i + 1) * width, :],
                    out_ref.at[r * width : (r + 1) * width, i * wide : (i + 1) * wide],
                )
            )
    return pairs


def weight_grads(rows, grad_rows, hidden, grad_pre, r, grad_ref):
    model = rows.shape[1]
    wide = grad_ref.shape[1]
    width = wide // 2
    grad_ref[:model, :] = lax.dot_general(
        rows, grad_pre[:, r * wide : (r + 1) * wide], FIRST, preferred_element_type=F32
    ).astype(BF16)
    value = lax.dot_general(
        hidden[:, r * width : (r + 1) * width], grad_rows, FIRST, preferred_element_type=F32
    ).astype(BF16)
    for i in range(model // wide):
        grad_ref[model + i * width : model + (i + 1) * width, :] = value[:, i * wide : (i + 1) * wide]


def expert_kernel(
    pieces, wire_hbm, *refs
):
    sources, back_hbm, grads_hbm = refs[:pieces], refs[pieces], refs[pieces + 1 : 2 * pieces + 1]
    grads = refs[2 * pieces + 1 : 3 * pieces + 1]
    (
        in_ref, out_ref, wire_ref, rows_ref, grad_rows_ref, hidden_ref, grad_pre_ref, sem, weights_sem, grad_sem
    ) = refs[3 * pieces + 1 :]
    wide = grads[0].shape[1]
    width = wide // 2
    arriving = pltpu.make_async_copy(wire_hbm, wire_ref, sem)
    arriving.start()
    weights = start_all(assembly(sources, in_ref, out_ref), weights_sem)
    arriving.wait()
    unweave_blocks(wire_ref, rows_ref, grad_rows_ref)
    wait_all(weights)
    rows = rows_ref[...]
    grad_rows = grad_rows_ref[...]
    preact = jnp.dot(rows, in_ref[...], preferred_element_type=F32)
    back = lax.dot_general(grad_rows, out_ref[...], LAST, preferred_element_type=F32)
    for r in range(pieces):
        gate_part = preact[:, r * wide : r * wide + width]
        up_part = preact[:, r * wide + width : (r + 1) * wide]
        back_part = back[:, r * width : (r + 1) * width]
        sig = jax.nn.sigmoid(gate_part)
        activated = gate_part * sig
        grad_gate = back_part * up_part * (sig * (1.0 + gate_part * (1.0 - sig)))
        hidden_ref[:, r * width : (r + 1) * width] = (activated * up_part).astype(BF16)
        grad_pre_ref[:, r * wide : r * wide + width] = grad_gate.astype(BF16)
        grad_pre_ref[:, r * wide + width : (r + 1) * wide] = (back_part * activated).astype(BF16)
    hidden = hidden_ref[...]
    grad_pre = grad_pre_ref[...]
    order = (1, 2, 3, 0)
    for r in order:
        weight_grads(rows, grad_rows, hidden, grad_pre, r, grads[r])
    leaving = start_all([(grads[r], grads_hbm[r]) for r in order], grad_sem)
    result = jnp.dot(hidden, out_ref[...], preferred_element_type=F32).astype(BF16)
    dx = lax.dot_general(grad_pre, in_ref[...], LAST, preferred_element_type=F32).astype(BF16)
    weave_blocks(result, dx, wire_ref)
    sending = pltpu.make_async_copy(wire_ref, back_hbm, sem)
    sending.start()
    sending.wait()
    wait_all(leaving)


def combine_kernel(
    wire_hbm, grad_hbm, ids_hbm, gates_hbm, mixed_ref, dx_ref, gate_grad_ref,
    wire_ref, result_ref, back_ref, grad_ref, ids_ref, gates_ref, sem,
):
    groups = result_ref.shape[0] // SLOTS
    copies = start_all(
        [(ids_hbm, ids_ref), (gates_hbm, gates_ref), (grad_hbm, grad_ref), (wire_hbm, wire_ref)], sem
    )
    wait_all(copies[:2])
    ids = ids_ref[...]
    per_token, count_tok = ids.shape
    held, gate, expert = routing(ids, gates_ref[...], groups)
    mix = jnp.concatenate([part.astype(F32) for part in three_parts(gate)] + [held], axis=1).T.astype(BF16)
    wait_all(copies[2:])
    unweave_blocks(wire_ref, result_ref, back_ref)
    result = result_ref[...]
    gate_rows = 3 * count_tok
    mixed = jnp.dot(mix[:gate_rows], result, preferred_element_type=F32)
    mixed_ref[...] = (
        mixed[:count_tok] + mixed[count_tok : 2 * count_tok] + mixed[2 * count_tok :]
    ).astype(BF16)
    dx_ref[...] = jnp.dot(mix[gate_rows:], back_ref[...], preferred_element_type=F32).astype(BF16)
    inner = lax.dot_general(result, grad_ref[...], LAST, preferred_element_type=F32) * held
    for k in range(per_token):
        hit = ids[k : k + 1, :] == expert
        gate_grad_ref[k : k + 1, :] = jnp.sum(jnp.where(hit, inner, 0.0), axis=0, keepdims=True)


def add_kernel(first_hbm, second_hbm, total_ref, first_ref, second_ref, sem):
    wait_all(start_all([(first_hbm, first_ref), (second_hbm, second_ref)], sem))
    total_ref[...] = (first_ref[...].astype(F32) + second_ref[...].astype(F32)).astype(BF16)


def reduce_kernel(*refs):
    pieces, (in_ref, out_ref) = refs[:-2], refs[-2:]
    wide = pieces[0].shape[1]
    width = wide // 2
    model = in_ref.shape[0] // 2

    def total(lower, size):
        value = pieces[0][lower : lower + size, :].astype(F32)
        for piece in pieces[1:]:
            value = value + piece[lower : lower + size, :].astype(F32)
        return value

    value = total(0, model)
    in_ref[pl.ds(0, model, stride=2), :] = value[:, :width]
    in_ref[pl.ds(1, model, stride=2), :] = value[:, width:]
    for i in range(model // wide):
        out_ref[:, i * wide : (i + 1) * wide] = total(model + i * width, width)


def per_device(tokens, grad_out, expert_ids, gates, w_in, w_out):
    count_tok, model = tokens.shape
    per_token = gates.shape[1]
    groups = lax.axis_size("expert")
    replicas = lax.axis_size("dp")
    width = w_out.shape[1]
    wide = 2 * width
    slots = groups * SLOTS
    wire = jax.ShapeDtypeStruct((groups * PIECE, model // 2), BF16)
    in_hbm = pl.BlockSpec(memory_space=pltpu.HBM)
    anywhere = pl.BlockSpec(memory_space=pl.ANY)
    in_vmem = pl.BlockSpec(memory_space=pltpu.VMEM)

    def room(mib):
        return pltpu.CompilerParams(vmem_limit_bytes=mib * MIB)


    def shift(x, by):
        return lax.ppermute(x, "dp", [(i, (i + by) % replicas) for i in range(replicas)])

    def held_in(x, space):
        return pltpu.with_memory_space_constraint(x, space)

    def exchange(x):
        x = x.reshape(groups, PIECE, model // 2)
        x = lax.all_to_all(x, "expert", split_axis=0, concat_axis=0, tiled=True)
        return x.reshape(groups * PIECE, model // 2)

    ids_t, gates_t = expert_ids.T, gates.T
    tokens_like = pltpu.VMEM(tokens.shape, BF16)
    ids_like = pltpu.VMEM(ids_t.shape, jnp.int32)
    gates_like = pltpu.VMEM(gates_t.shape, F32)
    piece = (model + width * (model // wide), wide)
    piece_like = pltpu.VMEM(piece, BF16)
    rows_like = pltpu.VMEM((slots, model), BF16)
    hidden_like = pltpu.VMEM((slots, replicas * width), BF16)
    grad_pre_like = pltpu.VMEM((slots, replicas * wide), BF16)
    wire_like = pltpu.VMEM(wire.shape, BF16)
    lines = 1 + model // wide
    inputs = [w_in.reshape(model, 2, width), w_out.reshape(width, model), tokens, grad_out, ids_t, gates_t]
    packed, send = pl.pallas_call(
        dispatch_kernel,
        out_shape=[pltpu.HBM(piece, BF16), pltpu.HBM(wire.shape, BF16)],
        in_specs=[in_hbm] * 6,
        out_specs=[in_hbm] * 2,
        scratch_shapes=[
            pltpu.VMEM((model, 2, width), BF16),
            piece_like, tokens_like, tokens_like, ids_like, gates_like, wire_like,
            pltpu.SemaphoreType.DMA((lines + 4,)),
            pltpu.SemaphoreType.DMA,
        ],
        compiler_params=room(10),
        name="dispatch",
    )(*[held_in(x, pltpu.HBM) for x in inputs])
    far = shift(packed, -2)
    far_late = pl.pallas_call(
        lambda far_hbm, out_ref, sem: wait_all(start_all([(far_hbm, out_ref)], sem)),
        out_shape=piece_like,
        in_specs=[anywhere],
        scratch_shapes=[pltpu.SemaphoreType.DMA((1,))],
        compiler_params=room(4),
        cost_estimate=pl.CostEstimate(flops=KEEP, bytes_accessed=0, transcendentals=0),
        name="keep",
    )(held_in(far, pltpu.HBM))
    arrived = exchange(send)

    back, own, grad_far, grad_next, grad_last = pl.pallas_call(
        lambda *refs: expert_kernel(replicas, *refs),
        out_shape=[pltpu.HBM(wire.shape, BF16)] + [pltpu.HBM(piece, BF16)] * replicas,
        in_specs=[in_hbm] + [anywhere] * replicas,
        out_specs=[in_hbm] * (1 + replicas),
        scratch_shapes=[piece_like] * replicas
        + [
            pltpu.VMEM((model, replicas * wide), BF16),
            pltpu.VMEM((replicas * width, model), BF16),
            wire_like, rows_like, rows_like, hidden_like, grad_pre_like,
            pltpu.SemaphoreType.DMA,
            pltpu.SemaphoreType.DMA((replicas * lines,)),
            pltpu.SemaphoreType.DMA((replicas,)),
        ],
        compiler_params=room(20),
        name="expert",
    )(arrived, held_in(packed, pltpu.HBM), far_late, shift(packed, -1), shift(packed, 1))
    returned = exchange(back)
    partial = pl.pallas_call(
        add_kernel,
        out_shape=jax.ShapeDtypeStruct(piece, BF16),
        in_specs=[in_hbm] * 2,
        scratch_shapes=[piece_like, piece_like, pltpu.SemaphoreType.DMA((2,))],
        compiler_params=room(6),
        cost_estimate=pl.CostEstimate(flops=BESIDE, bytes_accessed=0, transcendentals=0),
        name="add",
    )(held_in(own, pltpu.HBM), held_in(shift(grad_far, 2), pltpu.HBM))
    mixed, grad_tokens, gate_grad = pl.pallas_call(
        combine_kernel,
        out_shape=[
            jax.ShapeDtypeStruct(tokens.shape, BF16),
            jax.ShapeDtypeStruct(tokens.shape, BF16),
            jax.ShapeDtypeStruct((per_token, count_tok), F32),
        ],
        in_specs=[anywhere] * 4,
        scratch_shapes=[
            wire_like, rows_like, rows_like, tokens_like, ids_like, gates_like,
            pltpu.SemaphoreType.DMA((4,)),
        ],
        compiler_params=room(8),
        name="combine",
    )(returned, grad_out, ids_t, gates_t)
    partial, mixed = lax.optimization_barrier((partial, mixed))
    sum_in, sum_out = pl.pallas_call(
        reduce_kernel,
        out_shape=[
            jax.ShapeDtypeStruct((2 * model, width), F32),
            jax.ShapeDtypeStruct((width, model), F32),
        ],
        compiler_params=room(8),
        name="reduce",
    )(partial, shift(grad_next, 1), shift(grad_last, -1))
    return mixed, grad_tokens, gate_grad.T, sum_in.reshape(1, model, 2, width), sum_out[None]


def solution(mesh):
    in_specs = (
        P(("dp", "expert"), None),
        P(("dp", "expert"), None),
        P(("dp", "expert"), None),
        P(("dp", "expert"), None),
        P("expert", None, None, "dp"),
        P("expert", "dp", None),
    )
    out_specs = (
        P(("dp", "expert"), None),
        P(("dp", "expert"), None),
        P(("dp", "expert"), None),
        P("expert", None, None, "dp"),
        P("expert", "dp", None),
    )
    return jax.shard_map(
        per_device, mesh=mesh, in_specs=in_specs, out_specs=out_specs, check_vma=False
    )
```

```python
import jax
import jax.numpy as jnp
from jax import lax
from jax.experimental import pallas as pl
from jax.experimental.pallas import tpu as pltpu
from jax.sharding import PartitionSpec as P

BF16 = jnp.bfloat16
F32 = jnp.float32
SLOTS = 2
PIECE = 8
PEERS = 16
MIB = 1024 * 1024
KEEP = int(1.9e10)
BESIDE = int(1e11)
FIRST = (((0,), (0,)), ((), ()))
LAST = (((1,), (1,)), ((), ()))


def routing(ids, gates, groups):
    per_token, count_tok = ids.shape
    slots = groups * SLOTS
    line = lax.broadcasted_iota(jnp.int32, (slots, count_tok), 0)
    expert = line % groups
    place = line // groups
    named = jnp.zeros((slots, count_tok), F32)
    gate = jnp.zeros((slots, count_tok), F32)
    for k in range(per_token):
        hit = ids[k : k + 1, :] == expert
        named = jnp.where(hit, 1.0, named)
        gate = jnp.where(hit, gates[k : k + 1, :], gate)
    row = lax.broadcasted_iota(jnp.int32, (count_tok, count_tok), 0)
    col = lax.broadcasted_iota(jnp.int32, (count_tok, count_tok), 1)
    earlier = (row < col).astype(BF16)
    rank = jnp.dot(named.astype(BF16), earlier, preferred_element_type=F32)
    held = jnp.where(rank == place.astype(F32), named, 0.0)
    return held, held * gate, expert


def three_parts(x):
    high = x.astype(BF16)
    rest = x - high.astype(F32)
    mid = rest.astype(BF16)
    low = (rest - mid.astype(F32)).astype(BF16)
    return high, mid, low


def weave(back):
    size = PEERS * PIECE
    major, minor = (PIECE, PEERS) if back else (PEERS, PIECE)
    row = lax.broadcasted_iota(jnp.int32, (size, size), 0)
    col = lax.broadcasted_iota(jnp.int32, (size, size), 1)
    return ((row % minor) * major + row // minor == col).astype(BF16)


def weave_blocks(first, second, wire_ref):
    groups = first.shape[0] // SLOTS
    half = first.shape[1] // 2
    size = PEERS * PIECE
    permute = weave(False)
    for b in range(groups // PEERS):
        parts = []
        for array in (first, second):
            for c in range(SLOTS):
                lines = array[c * groups + b * PEERS : c * groups + (b + 1) * PEERS]
                parts += [lines[:, :half], lines[:, half:]]
        wire_ref[b * size : (b + 1) * size, :] = jnp.dot(
            permute, jnp.concatenate(parts, axis=0), preferred_element_type=F32
        ).astype(BF16)


def unweave_blocks(wire_ref, first_ref, second_ref):
    groups = first_ref.shape[0] // SLOTS
    half = first_ref.shape[1] // 2
    size = PEERS * PIECE
    permute = weave(True)
    for b in range(groups // PEERS):
        lines = jnp.dot(
            permute, wire_ref[b * size : (b + 1) * size, :], preferred_element_type=F32
        ).astype(BF16)
        i = 0
        for ref in (first_ref, second_ref):
            for c in range(SLOTS):
                for h in range(2):
                    ref[c * groups + b * PEERS : c * groups + (b + 1) * PEERS, h * half : (h + 1) * half] = lines[
                        i * PEERS : (i + 1) * PEERS
                    ]
                    i += 1


def start_all(pairs, sem):
    copies = [pltpu.make_async_copy(source, target, sem.at[i]) for i, (source, target) in enumerate(pairs)]
    for copy in copies:
        copy.start()
    return copies


def wait_all(copies):
    for copy in copies:
        copy.wait()


def dispatch_kernel(
    in_hbm, out_hbm, tokens_hbm, grad_hbm, ids_hbm, gates_hbm, packed_hbm, send_hbm,
    raw_ref, packed_ref, tokens_ref, grad_ref, ids_ref, gates_ref, wire_ref, sem, wire_sem,
):
    model = in_hbm.shape[0]
    groups = send_hbm.shape[0] // PIECE
    wide = packed_ref.shape[1]
    width = wide // 2
    pairs = [(ids_hbm, ids_ref), (gates_hbm, gates_ref), (tokens_hbm, tokens_ref), (grad_hbm, grad_ref)]
    small = len(pairs)
    pairs.append((in_hbm, raw_ref))
    for i in range(model // wide):
        pairs.append(
            (
                out_hbm.at[:, i * wide : (i + 1) * wide],
                packed_ref.at[model + i * width : model + (i + 1) * width, :],
            )
        )
    copies = start_all(pairs, sem)
    wait_all(copies[:small])
    held, gate, _ = routing(ids_ref[...], gates_ref[...], groups)
    rows = jnp.dot(held.astype(BF16), tokens_ref[...], preferred_element_type=F32).astype(BF16)
    grad = grad_ref[...]
    grad_rows = jnp.dot(
        jnp.concatenate(three_parts(gate), axis=1),
        jnp.concatenate([grad, grad, grad], axis=0),
        preferred_element_type=F32,
    ).astype(BF16)
    weave_blocks(rows, grad_rows, wire_ref)
    sending = pltpu.make_async_copy(wire_ref, send_hbm, wire_sem)
    sending.start()
    wait_all(copies[small:])
    packed_ref[:model, :] = raw_ref[...].reshape(model, wide)
    leaving = pltpu.make_async_copy(packed_ref, packed_hbm, sem.at[0])
    leaving.start()
    sending.wait()
    leaving.wait()


def assembly(sources, in_ref, out_ref):
    model = in_ref.shape[0]
    wide = sources[0].shape[1]
    width = wide // 2
    pairs = []
    for r, source in enumerate(sources):
        pairs.append((source.at[:model, :], in_ref.at[:, r * wide : (r + 1) * wide]))
        for i in range(model // wide):
            pairs.append(
                (
                    source.at[model + i * width : model + (i + 1) * width, :],
                    out_ref.at[r * width : (r + 1) * width, i * wide : (i + 1) * wide],
                )
            )
    return pairs


def weight_grads(rows, grad_rows, hidden, grad_pre, r, grad_ref):
    model = rows.shape[1]
    wide = grad_ref.shape[1]
    width = wide // 2
    grad_ref[:model, :] = lax.dot_general(
        rows, grad_pre[:, r * wide : (r + 1) * wide], FIRST, preferred_element_type=F32
    ).astype(BF16)
    value = lax.dot_general(
        hidden[:, r * width : (r + 1) * width], grad_rows, FIRST, preferred_element_type=F32
    ).astype(BF16)
    for i in range(model // wide):
        grad_ref[model + i * width : model + (i + 1) * width, :] = value[:, i * wide : (i + 1) * wide]


def expert_kernel(
    pieces, wire_hbm, *refs
):
    sources, back_hbm, grads_hbm = refs[:pieces], refs[pieces], refs[pieces + 1 : 2 * pieces + 1]
    grads = refs[2 * pieces + 1 : 3 * pieces + 1]
    (
        in_ref, out_ref, wire_ref, rows_ref, grad_rows_ref, hidden_ref, grad_pre_ref, sem, weights_sem, grad_sem
    ) = refs[3 * pieces + 1 :]
    wide = grads[0].shape[1]
    width = wide // 2
    arriving = pltpu.make_async_copy(wire_hbm, wire_ref, sem)
    arriving.start()
    weights = start_all(assembly(sources, in_ref, out_ref), weights_sem)
    arriving.wait()
    unweave_blocks(wire_ref, rows_ref, grad_rows_ref)
    wait_all(weights)
    rows = rows_ref[...]
    grad_rows = grad_rows_ref[...]
    preact = jnp.dot(rows, in_ref[...], preferred_element_type=F32)
    back = lax.dot_general(grad_rows, out_ref[...], LAST, preferred_element_type=F32)
    for r in range(pieces):
        gate_part = preact[:, r * wide : r * wide + width]
        up_part = preact[:, r * wide + width : (r + 1) * wide]
        back_part = back[:, r * width : (r + 1) * width]
        sig = jax.nn.sigmoid(gate_part)
        activated = gate_part * sig
        grad_gate = back_part * up_part * (sig * (1.0 + gate_part * (1.0 - sig)))
        hidden_ref[:, r * width : (r + 1) * width] = (activated * up_part).astype(BF16)
        grad_pre_ref[:, r * wide : r * wide + width] = grad_gate.astype(BF16)
        grad_pre_ref[:, r * wide + width : (r + 1) * wide] = (back_part * activated).astype(BF16)
    hidden = hidden_ref[...]
    grad_pre = grad_pre_ref[...]
    order = (1, 2, 3, 0)
    for r in order:
        weight_grads(rows, grad_rows, hidden, grad_pre, r, grads[r])
    leaving = start_all([(grads[r], grads_hbm[r]) for r in order], grad_sem)
    result = jnp.dot(hidden, out_ref[...], preferred_element_type=F32).astype(BF16)
    dx = lax.dot_general(grad_pre, in_ref[...], LAST, preferred_element_type=F32).astype(BF16)
    weave_blocks(result, dx, wire_ref)
    sending = pltpu.make_async_copy(wire_ref, back_hbm, sem)
    sending.start()
    sending.wait()
    wait_all(leaving)


def combine_kernel(
    wire_hbm, grad_hbm, ids_hbm, gates_hbm, mixed_ref, dx_ref, gate_grad_ref,
    wire_ref, result_ref, back_ref, grad_ref, ids_ref, gates_ref, sem,
):
    groups = result_ref.shape[0] // SLOTS
    copies = start_all(
        [(ids_hbm, ids_ref), (gates_hbm, gates_ref), (grad_hbm, grad_ref), (wire_hbm, wire_ref)], sem
    )
    wait_all(copies[:2])
    ids = ids_ref[...]
    per_token, count_tok = ids.shape
    held, gate, expert = routing(ids, gates_ref[...], groups)
    mix = jnp.concatenate([part.astype(F32) for part in three_parts(gate)] + [held], axis=1).T.astype(BF16)
    wait_all(copies[2:])
    unweave_blocks(wire_ref, result_ref, back_ref)
    result = result_ref[...]
    gate_rows = 3 * count_tok
    mixed = jnp.dot(mix[:gate_rows], result, preferred_element_type=F32)
    mixed_ref[...] = (
        mixed[:count_tok] + mixed[count_tok : 2 * count_tok] + mixed[2 * count_tok :]
    ).astype(BF16)
    dx_ref[...] = jnp.dot(mix[gate_rows:], back_ref[...], preferred_element_type=F32).astype(BF16)
    inner = lax.dot_general(result, grad_ref[...], LAST, preferred_element_type=F32) * held
    for k in range(per_token):
        hit = ids[k : k + 1, :] == expert
        gate_grad_ref[k : k + 1, :] = jnp.sum(jnp.where(hit, inner, 0.0), axis=0, keepdims=True)


def add_kernel(first_hbm, second_hbm, total_ref, first_ref, second_ref, sem):
    wait_all(start_all([(first_hbm, first_ref), (second_hbm, second_ref)], sem))
    total_ref[...] = (first_ref[...].astype(F32) + second_ref[...].astype(F32)).astype(BF16)


def reduce_kernel(*refs):
    pieces, (in_ref, out_ref) = refs[:-2], refs[-2:]
    wide = pieces[0].shape[1]
    width = wide // 2
    model = in_ref.shape[0] // 2

    def total(lower, size):
        value = pieces[0][lower : lower + size, :].astype(F32)
        for piece in pieces[1:]:
            value = value + piece[lower : lower + size, :].astype(F32)
        return value

    value = total(0, model)
    in_ref[pl.ds(0, model, stride=2), :] = value[:, :width]
    in_ref[pl.ds(1, model, stride=2), :] = value[:, width:]
    for i in range(model // wide):
        out_ref[:, i * wide : (i + 1) * wide] = total(model + i * width, width)


def per_device(tokens, grad_out, expert_ids, gates, w_in, w_out):
    count_tok, model = tokens.shape
    per_token = gates.shape[1]
    groups = lax.axis_size("expert")
    replicas = lax.axis_size("dp")
    width = w_out.shape[1]
    wide = 2 * width
    slots = groups * SLOTS
    wire = jax.ShapeDtypeStruct((groups * PIECE, model // 2), BF16)
    in_hbm = pl.BlockSpec(memory_space=pltpu.HBM)
    anywhere = pl.BlockSpec(memory_space=pl.ANY)
    in_vmem = pl.BlockSpec(memory_space=pltpu.VMEM)

    def room(mib):
        return pltpu.CompilerParams(vmem_limit_bytes=mib * MIB)


    def shift(x, by):
        return lax.ppermute(x, "dp", [(i, (i + by) % replicas) for i in range(replicas)])

    def held_in(x, space):
        return pltpu.with_memory_space_constraint(x, space)

    def exchange(x):
        x = x.reshape(groups, PIECE, model // 2)
        x = lax.all_to_all(x, "expert", split_axis=0, concat_axis=0, tiled=True)
        return x.reshape(groups * PIECE, model // 2)

    ids_t, gates_t = expert_ids.T, gates.T
    tokens_like = pltpu.VMEM(tokens.shape, BF16)
    ids_like = pltpu.VMEM(ids_t.shape, jnp.int32)
    gates_like = pltpu.VMEM(gates_t.shape, F32)
    piece = (model + width * (model // wide), wide)
    piece_like = pltpu.VMEM(piece, BF16)
    rows_like = pltpu.VMEM((slots, model), BF16)
    hidden_like = pltpu.VMEM((slots, replicas * width), BF16)
    grad_pre_like = pltpu.VMEM((slots, replicas * wide), BF16)
    wire_like = pltpu.VMEM(wire.shape, BF16)
    lines = 1 + model // wide
    inputs = [w_in.reshape(model, 2, width), w_out.reshape(width, model), tokens, grad_out, ids_t, gates_t]
    packed, send = pl.pallas_call(
        dispatch_kernel,
        out_shape=[pltpu.HBM(piece, BF16), pltpu.HBM(wire.shape, BF16)],
        in_specs=[in_hbm] * 6,
        out_specs=[in_hbm] * 2,
        scratch_shapes=[
            pltpu.VMEM((model, 2, width), BF16),
            piece_like, tokens_like, tokens_like, ids_like, gates_like, wire_like,
            pltpu.SemaphoreType.DMA((lines + 4,)),
            pltpu.SemaphoreType.DMA,
        ],
        compiler_params=room(10),
        name="dispatch",
    )(*[held_in(x, pltpu.HBM) for x in inputs])
    last = shift(packed, 1)
    last_near = pl.pallas_call(
        lambda far_hbm, out_ref, sem: wait_all(start_all([(far_hbm, out_ref)], sem)),
        out_shape=piece_like,
        in_specs=[anywhere],
        scratch_shapes=[pltpu.SemaphoreType.DMA((1,))],
        compiler_params=room(4),
        cost_estimate=pl.CostEstimate(flops=KEEP, bytes_accessed=0, transcendentals=0),
        name="keep",
    )(held_in(last, pltpu.HBM))
    arrived = exchange(send)

    back, own, grad_far, grad_next, grad_last = pl.pallas_call(
        lambda *refs: expert_kernel(replicas, *refs),
        out_shape=[pltpu.HBM(wire.shape, BF16)] + [pltpu.HBM(piece, BF16)] * replicas,
        in_specs=[in_hbm] + [anywhere] * replicas,
        out_specs=[in_hbm] * (1 + replicas),
        scratch_shapes=[piece_like] * replicas
        + [
            pltpu.VMEM((model, replicas * wide), BF16),
            pltpu.VMEM((replicas * width, model), BF16),
            wire_like, rows_like, rows_like, hidden_like, grad_pre_like,
            pltpu.SemaphoreType.DMA,
            pltpu.SemaphoreType.DMA((replicas * lines,)),
            pltpu.SemaphoreType.DMA((replicas,)),
        ],
        compiler_params=room(20),
        name="expert",
    )(arrived, held_in(packed, pltpu.HBM), shift(last, 1), shift(packed, -1), last_near)
    returned = exchange(back)
    partial = pl.pallas_call(
        add_kernel,
        out_shape=jax.ShapeDtypeStruct(piece, BF16),
        in_specs=[in_hbm] * 2,
        scratch_shapes=[piece_like, piece_like, pltpu.SemaphoreType.DMA((2,))],
        compiler_params=room(6),
        cost_estimate=pl.CostEstimate(flops=BESIDE, bytes_accessed=0, transcendentals=0),
        name="add",
    )(held_in(own, pltpu.HBM), held_in(shift(grad_far, 2), pltpu.HBM))
    mixed, grad_tokens, gate_grad = pl.pallas_call(
        combine_kernel,
        out_shape=[
            jax.ShapeDtypeStruct(tokens.shape, BF16),
            jax.ShapeDtypeStruct(tokens.shape, BF16),
            jax.ShapeDtypeStruct((per_token, count_tok), F32),
        ],
        in_specs=[anywhere] * 4,
        scratch_shapes=[
            wire_like, rows_like, rows_like, tokens_like, ids_like, gates_like,
            pltpu.SemaphoreType.DMA((4,)),
        ],
        compiler_params=room(8),
        name="combine",
    )(returned, grad_out, ids_t, gates_t)
    partial, mixed = lax.optimization_barrier((partial, mixed))
    sum_in, sum_out = pl.pallas_call(
        reduce_kernel,
        out_shape=[
            jax.ShapeDtypeStruct((2 * model, width), F32),
            jax.ShapeDtypeStruct((width, model), F32),
        ],
        compiler_params=room(8),
        name="reduce",
    )(partial, shift(grad_last, -1), shift(grad_next, 1))
    return mixed, grad_tokens, gate_grad.T, sum_in.reshape(1, model, 2, width), sum_out[None]


def solution(mesh):
    in_specs = (
        P(("dp", "expert"), None),
        P(("dp", "expert"), None),
        P(("dp", "expert"), None),
        P(("dp", "expert"), None),
        P("expert", None, None, "dp"),
        P("expert", "dp", None),
    )
    out_specs = (
        P(("dp", "expert"), None),
        P(("dp", "expert"), None),
        P(("dp", "expert"), None),
        P("expert", None, None, "dp"),
        P("expert", "dp", None),
    )
    return jax.shard_map(
        per_device, mesh=mesh, in_specs=in_specs, out_specs=out_specs, check_vma=False
    )
```

```python
import jax
import jax.numpy as jnp
from jax import lax
from jax.experimental import pallas as pl
from jax.experimental.pallas import tpu as pltpu
from jax.sharding import PartitionSpec as P

BF16 = jnp.bfloat16
F32 = jnp.float32
SLOTS = 2
PIECE = 8
PEERS = 16
MIB = 1024 * 1024
KEEP = int(1.9e10)
BESIDE = int(1e11)
FIRST = (((0,), (0,)), ((), ()))
LAST = (((1,), (1,)), ((), ()))


def routing(ids, gates, groups):
    per_token, count_tok = ids.shape
    slots = groups * SLOTS
    line = lax.broadcasted_iota(jnp.int32, (slots, count_tok), 0)
    expert = line % groups
    place = line // groups
    named = jnp.zeros((slots, count_tok), F32)
    gate = jnp.zeros((slots, count_tok), F32)
    for k in range(per_token):
        hit = ids[k : k + 1, :] == expert
        named = jnp.where(hit, 1.0, named)
        gate = jnp.where(hit, gates[k : k + 1, :], gate)
    row = lax.broadcasted_iota(jnp.int32, (count_tok, count_tok), 0)
    col = lax.broadcasted_iota(jnp.int32, (count_tok, count_tok), 1)
    earlier = (row < col).astype(BF16)
    rank = jnp.dot(named.astype(BF16), earlier, preferred_element_type=F32)
    held = jnp.where(rank == place.astype(F32), named, 0.0)
    return held, held * gate, expert


def three_parts(x):
    high = x.astype(BF16)
    rest = x - high.astype(F32)
    mid = rest.astype(BF16)
    low = (rest - mid.astype(F32)).astype(BF16)
    return high, mid, low


def weave(back):
    size = PEERS * PIECE
    major, minor = (PIECE, PEERS) if back else (PEERS, PIECE)
    row = lax.broadcasted_iota(jnp.int32, (size, size), 0)
    col = lax.broadcasted_iota(jnp.int32, (size, size), 1)
    return ((row % minor) * major + row // minor == col).astype(BF16)


def weave_blocks(first, second, wire_ref):
    groups = first.shape[0] // SLOTS
    half = first.shape[1] // 2
    size = PEERS * PIECE
    permute = weave(False)
    for b in range(groups // PEERS):
        parts = []
        for array in (first, second):
            for c in range(SLOTS):
                lines = array[c * groups + b * PEERS : c * groups + (b + 1) * PEERS]
                parts += [lines[:, :half], lines[:, half:]]
        wire_ref[b * size : (b + 1) * size, :] = jnp.dot(
            permute, jnp.concatenate(parts, axis=0), preferred_element_type=F32
        ).astype(BF16)


def unweave_blocks(wire_ref, first_ref, second_ref):
    groups = first_ref.shape[0] // SLOTS
    half = first_ref.shape[1] // 2
    size = PEERS * PIECE
    permute = weave(True)
    for b in range(groups // PEERS):
        lines = jnp.dot(
            permute, wire_ref[b * size : (b + 1) * size, :], preferred_element_type=F32
        ).astype(BF16)
        i = 0
        for ref in (first_ref, second_ref):
            for c in range(SLOTS):
                for h in range(2):
                    ref[c * groups + b * PEERS : c * groups + (b + 1) * PEERS, h * half : (h + 1) * half] = lines[
                        i * PEERS : (i + 1) * PEERS
                    ]
                    i += 1


def start_all(pairs, sem):
    copies = [pltpu.make_async_copy(source, target, sem.at[i]) for i, (source, target) in enumerate(pairs)]
    for copy in copies:
        copy.start()
    return copies


def wait_all(copies):
    for copy in copies:
        copy.wait()


def dispatch_kernel(
    in_hbm, out_hbm, tokens_hbm, grad_hbm, ids_hbm, gates_hbm, packed_hbm, send_hbm,
    raw_ref, packed_ref, tokens_ref, grad_ref, ids_ref, gates_ref, wire_ref, sem, wire_sem,
):
    model = in_hbm.shape[0]
    groups = send_hbm.shape[0] // PIECE
    wide = packed_ref.shape[1]
    width = wide // 2
    pairs = [(ids_hbm, ids_ref), (gates_hbm, gates_ref), (tokens_hbm, tokens_ref), (grad_hbm, grad_ref)]
    small = len(pairs)
    pairs.append((in_hbm, raw_ref))
    for i in range(model // wide):
        pairs.append(
            (
                out_hbm.at[:, i * wide : (i + 1) * wide],
                packed_ref.at[model + i * width : model + (i + 1) * width, :],
            )
        )
    copies = start_all(pairs, sem)
    wait_all(copies[:small])
    held, gate, _ = routing(ids_ref[...], gates_ref[...], groups)
    rows = jnp.dot(held.astype(BF16), tokens_ref[...], preferred_element_type=F32).astype(BF16)
    grad = grad_ref[...]
    grad_rows = jnp.dot(
        jnp.concatenate(three_parts(gate), axis=1),
        jnp.concatenate([grad, grad, grad], axis=0),
        preferred_element_type=F32,
    ).astype(BF16)
    weave_blocks(rows, grad_rows, wire_ref)
    sending = pltpu.make_async_copy(wire_ref, send_hbm, wire_sem)
    sending.start()
    wait_all(copies[small:])
    packed_ref[:model, :] = raw_ref[...].reshape(model, wide)
    leaving = pltpu.make_async_copy(packed_ref, packed_hbm, sem.at[0])
    leaving.start()
    sending.wait()
    leaving.wait()


def assembly(sources, in_ref, out_ref):
    model = in_ref.shape[0]
    wide = sources[0].shape[1]
    width = wide // 2
    pairs = []
    for r, source in enumerate(sources):
        pairs.append((source.at[:model, :], in_ref.at[:, r * wide : (r + 1) * wide]))
        for i in range(model // wide):
            pairs.append(
                (
                    source.at[model + i * width : model + (i + 1) * width, :],
                    out_ref.at[r * width : (r + 1) * width, i * wide : (i + 1) * wide],
                )
            )
    return pairs


def weight_grads(rows, grad_rows, hidden, grad_pre, r, grad_ref):
    model = rows.shape[1]
    wide = grad_ref.shape[1]
    width = wide // 2
    grad_ref[:model, :] = lax.dot_general(
        rows, grad_pre[:, r * wide : (r + 1) * wide], FIRST, preferred_element_type=F32
    ).astype(BF16)
    value = lax.dot_general(
        hidden[:, r * width : (r + 1) * width], grad_rows, FIRST, preferred_element_type=F32
    ).astype(BF16)
    for i in range(model // wide):
        grad_ref[model + i * width : model + (i + 1) * width, :] = value[:, i * wide : (i + 1) * wide]


def expert_kernel(
    pieces, wire_hbm, *refs
):
    sources = refs[:pieces]
    (
        back_hbm, rows_hbm, grad_rows_hbm, hidden_hbm, grad_pre_hbm, grad_hbm,
        grad_ref, in_ref, out_ref, wire_ref, rows_ref, grad_rows_ref, hidden_ref, grad_pre_ref,
        sem, weights_sem, grad_sem, keep_sem,
    ) = refs[pieces:]
    wide = grad_ref.shape[1]
    width = wide // 2
    arriving = pltpu.make_async_copy(wire_hbm, wire_ref, sem)
    arriving.start()
    weights = start_all(assembly(sources, in_ref, out_ref), weights_sem)
    arriving.wait()
    unweave_blocks(wire_ref, rows_ref, grad_rows_ref)
    keeping = start_all([(rows_ref, rows_hbm), (grad_rows_ref, grad_rows_hbm)], keep_sem)
    wait_all(weights)
    rows = rows_ref[...]
    grad_rows = grad_rows_ref[...]
    preact = jnp.dot(rows, in_ref[...], preferred_element_type=F32)
    back = lax.dot_general(grad_rows, out_ref[...], LAST, preferred_element_type=F32)
    for r in range(pieces):
        gate_part = preact[:, r * wide : r * wide + width]
        up_part = preact[:, r * wide + width : (r + 1) * wide]
        back_part = back[:, r * width : (r + 1) * width]
        sig = jax.nn.sigmoid(gate_part)
        activated = gate_part * sig
        grad_gate = back_part * up_part * (sig * (1.0 + gate_part * (1.0 - sig)))
        hidden_ref[:, r * width : (r + 1) * width] = (activated * up_part).astype(BF16)
        grad_pre_ref[:, r * wide : r * wide + width] = grad_gate.astype(BF16)
        grad_pre_ref[:, r * wide + width : (r + 1) * wide] = (back_part * activated).astype(BF16)
    hidden = hidden_ref[...]
    grad_pre = grad_pre_ref[...]
    for i, pair in enumerate([(hidden_ref, hidden_hbm), (grad_pre_ref, grad_pre_hbm)]):
        keeping.append(pltpu.make_async_copy(*pair, keep_sem.at[2 + i]))
        keeping[-1].start()
    weight_grads(rows, grad_rows, hidden, grad_pre, 1, grad_ref)
    leaving = pltpu.make_async_copy(grad_ref, grad_hbm, grad_sem)
    leaving.start()
    result = jnp.dot(hidden, out_ref[...], preferred_element_type=F32).astype(BF16)
    dx = lax.dot_general(grad_pre, in_ref[...], LAST, preferred_element_type=F32).astype(BF16)
    weave_blocks(result, dx, wire_ref)
    sending = pltpu.make_async_copy(wire_ref, back_hbm, sem)
    sending.start()
    sending.wait()
    leaving.wait()
    wait_all(keeping)


def weights_kernel(rows_ref, grad_rows_ref, hidden_ref, grad_pre_ref, own_ref, next_ref, last_ref):
    operands = rows_ref[...], grad_rows_ref[...], hidden_ref[...], grad_pre_ref[...]
    weight_grads(*operands, 3, last_ref)
    weight_grads(*operands, 2, next_ref)
    weight_grads(*operands, 0, own_ref)


def combine_kernel(
    wire_hbm, grad_hbm, ids_hbm, gates_hbm, mixed_ref, dx_ref, gate_grad_ref,
    wire_ref, result_ref, back_ref, grad_ref, ids_ref, gates_ref, sem,
):
    groups = result_ref.shape[0] // SLOTS
    copies = start_all(
        [(ids_hbm, ids_ref), (gates_hbm, gates_ref), (grad_hbm, grad_ref), (wire_hbm, wire_ref)], sem
    )
    wait_all(copies[:2])
    ids = ids_ref[...]
    per_token, count_tok = ids.shape
    held, gate, expert = routing(ids, gates_ref[...], groups)
    mix = jnp.concatenate([part.astype(F32) for part in three_parts(gate)] + [held], axis=1).T.astype(BF16)
    wait_all(copies[2:])
    unweave_blocks(wire_ref, result_ref, back_ref)
    result = result_ref[...]
    gate_rows = 3 * count_tok
    mixed = jnp.dot(mix[:gate_rows], result, preferred_element_type=F32)
    mixed_ref[...] = (
        mixed[:count_tok] + mixed[count_tok : 2 * count_tok] + mixed[2 * count_tok :]
    ).astype(BF16)
    dx_ref[...] = jnp.dot(mix[gate_rows:], back_ref[...], preferred_element_type=F32).astype(BF16)
    inner = lax.dot_general(result, grad_ref[...], LAST, preferred_element_type=F32) * held
    for k in range(per_token):
        hit = ids[k : k + 1, :] == expert
        gate_grad_ref[k : k + 1, :] = jnp.sum(jnp.where(hit, inner, 0.0), axis=0, keepdims=True)


def add_kernel(first_hbm, second_hbm, total_ref, first_ref, second_ref, sem):
    wait_all(start_all([(first_hbm, first_ref), (second_hbm, second_ref)], sem))
    total_ref[...] = (first_ref[...].astype(F32) + second_ref[...].astype(F32)).astype(BF16)


def reduce_kernel(*refs):
    pieces, (in_ref, out_ref) = refs[:-2], refs[-2:]
    wide = pieces[0].shape[1]
    width = wide // 2
    model = in_ref.shape[0] // 2

    def total(lower, size):
        value = pieces[0][lower : lower + size, :].astype(F32)
        for piece in pieces[1:]:
            value = value + piece[lower : lower + size, :].astype(F32)
        return value

    value = total(0, model)
    in_ref[pl.ds(0, model, stride=2), :] = value[:, :width]
    in_ref[pl.ds(1, model, stride=2), :] = value[:, width:]
    for i in range(model // wide):
        out_ref[:, i * wide : (i + 1) * wide] = total(model + i * width, width)


def per_device(tokens, grad_out, expert_ids, gates, w_in, w_out):
    count_tok, model = tokens.shape
    per_token = gates.shape[1]
    groups = lax.axis_size("expert")
    replicas = lax.axis_size("dp")
    width = w_out.shape[1]
    wide = 2 * width
    slots = groups * SLOTS
    wire = jax.ShapeDtypeStruct((groups * PIECE, model // 2), BF16)
    in_hbm = pl.BlockSpec(memory_space=pltpu.HBM)
    anywhere = pl.BlockSpec(memory_space=pl.ANY)
    in_vmem = pl.BlockSpec(memory_space=pltpu.VMEM)

    def room(mib):
        return pltpu.CompilerParams(vmem_limit_bytes=mib * MIB)


    def shift(x, by):
        return lax.ppermute(x, "dp", [(i, (i + by) % replicas) for i in range(replicas)])

    def held_in(x, space):
        return pltpu.with_memory_space_constraint(x, space)

    def exchange(x):
        x = x.reshape(groups, PIECE, model // 2)
        x = lax.all_to_all(x, "expert", split_axis=0, concat_axis=0, tiled=True)
        return x.reshape(groups * PIECE, model // 2)

    ids_t, gates_t = expert_ids.T, gates.T
    tokens_like = pltpu.VMEM(tokens.shape, BF16)
    ids_like = pltpu.VMEM(ids_t.shape, jnp.int32)
    gates_like = pltpu.VMEM(gates_t.shape, F32)
    piece = (model + width * (model // wide), wide)
    piece_like = pltpu.VMEM(piece, BF16)
    rows_like = pltpu.VMEM((slots, model), BF16)
    hidden_like = pltpu.VMEM((slots, replicas * width), BF16)
    grad_pre_like = pltpu.VMEM((slots, replicas * wide), BF16)
    wire_like = pltpu.VMEM(wire.shape, BF16)
    lines = 1 + model // wide
    inputs = [w_in.reshape(model, 2, width), w_out.reshape(width, model), tokens, grad_out, ids_t, gates_t]
    packed, send = pl.pallas_call(
        dispatch_kernel,
        out_shape=[pltpu.HBM(piece, BF16), pltpu.HBM(wire.shape, BF16)],
        in_specs=[in_hbm] * 6,
        out_specs=[in_hbm] * 2,
        scratch_shapes=[
            pltpu.VMEM((model, 2, width), BF16),
            piece_like, tokens_like, tokens_like, ids_like, gates_like, wire_like,
            pltpu.SemaphoreType.DMA((lines + 4,)),
            pltpu.SemaphoreType.DMA,
        ],
        compiler_params=room(10),
        name="dispatch",
    )(*[held_in(x, pltpu.HBM) for x in inputs])
    last = shift(packed, 1)
    last_near = pl.pallas_call(
        lambda far_hbm, out_ref, sem: wait_all(start_all([(far_hbm, out_ref)], sem)),
        out_shape=piece_like,
        in_specs=[anywhere],
        scratch_shapes=[pltpu.SemaphoreType.DMA((1,))],
        compiler_params=room(4),
        cost_estimate=pl.CostEstimate(flops=KEEP, bytes_accessed=0, transcendentals=0),
        name="keep",
    )(held_in(last, pltpu.HBM))
    arrived = exchange(send)

    back, rows, grad_rows, hidden, grad_pre, grad_far = pl.pallas_call(
        lambda *refs: expert_kernel(replicas, *refs),
        out_shape=[
            pltpu.HBM(x.shape, BF16) for x in (wire, rows_like, rows_like, hidden_like, grad_pre_like, piece_like)
        ],
        in_specs=[in_hbm] + [anywhere] * replicas,
        out_specs=[in_hbm] * 6,
        scratch_shapes=[
            piece_like,
            pltpu.VMEM((model, replicas * wide), BF16),
            pltpu.VMEM((replicas * width, model), BF16),
            wire_like, rows_like, rows_like, hidden_like, grad_pre_like,
            pltpu.SemaphoreType.DMA,
            pltpu.SemaphoreType.DMA((replicas * lines,)),
            pltpu.SemaphoreType.DMA,
            pltpu.SemaphoreType.DMA((4,)),
        ],
        compiler_params=room(20),
        name="expert",
    )(arrived, held_in(packed, pltpu.HBM), shift(last, 1), shift(packed, -1), last_near)
    own, grad_next, grad_last = pl.pallas_call(
        weights_kernel,
        out_shape=[jax.ShapeDtypeStruct(piece, BF16)] * 3,
        compiler_params=room(10),
        name="weights",
    )(rows, grad_rows, hidden, grad_pre)
    returned = exchange(back)
    partial = pl.pallas_call(
        add_kernel,
        out_shape=jax.ShapeDtypeStruct(piece, BF16),
        in_specs=[in_hbm] * 2,
        scratch_shapes=[piece_like, piece_like, pltpu.SemaphoreType.DMA((2,))],
        compiler_params=room(6),
        cost_estimate=pl.CostEstimate(flops=BESIDE, bytes_accessed=0, transcendentals=0),
        name="add",
    )(held_in(own, pltpu.HBM), held_in(shift(grad_far, 2), pltpu.HBM))
    mixed, grad_tokens, gate_grad = pl.pallas_call(
        combine_kernel,
        out_shape=[
            jax.ShapeDtypeStruct(tokens.shape, BF16),
            jax.ShapeDtypeStruct(tokens.shape, BF16),
            jax.ShapeDtypeStruct((per_token, count_tok), F32),
        ],
        in_specs=[anywhere] * 4,
        scratch_shapes=[
            wire_like, rows_like, rows_like, tokens_like, ids_like, gates_like,
            pltpu.SemaphoreType.DMA((4,)),
        ],
        compiler_params=room(8),
        name="combine",
    )(returned, grad_out, ids_t, gates_t)
    partial, mixed = lax.optimization_barrier((partial, mixed))
    sum_in, sum_out = pl.pallas_call(
        reduce_kernel,
        out_shape=[
            jax.ShapeDtypeStruct((2 * model, width), F32),
            jax.ShapeDtypeStruct((width, model), F32),
        ],
        compiler_params=room(8),
        name="reduce",
    )(partial, shift(grad_last, -1), shift(grad_next, 1))
    return mixed, grad_tokens, gate_grad.T, sum_in.reshape(1, model, 2, width), sum_out[None]


def solution(mesh):
    in_specs = (
        P(("dp", "expert"), None),
        P(("dp", "expert"), None),
        P(("dp", "expert"), None),
        P(("dp", "expert"), None),
        P("expert", None, None, "dp"),
        P("expert", "dp", None),
    )
    out_specs = (
        P(("dp", "expert"), None),
        P(("dp", "expert"), None),
        P(("dp", "expert"), None),
        P("expert", None, None, "dp"),
        P("expert", "dp", None),
    )
    return jax.shard_map(
        per_device, mesh=mesh, in_specs=in_specs, out_specs=out_specs, check_vma=False
    )
```
